32 devices in a mesh: groups: 2 (over x), grid: 8 (over z, y), rep: 2 (over core).
Axes of the slice: x: 2, y: 2, z: 4, core: 2. Of those that a mesh axis runs over, the one named last changes fastest.
Arguments:
- feats: bfloat16 [14336, 256], P(('groups', 'grid')), parts along dimension 0, may hold values from -6 to 6
- msg_weight: bfloat16 [256, 256], replicated, may hold values from -0.375 to 0.375
- tiles: bfloat16 [16, 2, 1, 896, 896], P(('groups', 'grid'), 'rep'), parts along dimension 0, may hold values from -0.1875 to 0.1875
- tile_step: int32 [16, 2, 1], P(('groups', 'grid'), 'rep'), parts along dimension 0, may hold values from 0 to 3, as said below
- tile_count: int32 [16, 2, 1], P(('groups', 'grid'), 'rep'), parts along dimension 0, may hold values from 0 to 63, as said below
- node_type: int32 [14336], P(('groups', 'grid')), parts along dimension 0, may hold values from 0 to 7
- expert_up: bfloat16 [8, 256, 512], replicated, may hold values from -0.375 to 0.375
- expert_down: bfloat16 [8, 512, 256], replicated, may hold values from -0.25 to 0.25
- out_grad: bfloat16 [14336, 256], P(('groups', 'grid', 'rep')), parts along dimension 0, may hold values from -6 to 6
Outputs:
- updated: bfloat16 [14336, 256], P(('groups', 'grid', 'rep')), parts along dimension 0
- feats_grad: bfloat16 [14336, 256], P(('groups', 'grid', 'rep')), parts along dimension 0
- msg_weight_grad: float32 [512, 256], P('groups'), parts along dimension 0
The draws below stay inside these ranges and needn't reach their ends.
There are 2 independent parts, one for each index of `groups`. The reference program is written for one: setup_inputs(seed, part) draws one part's arguments, and reference() takes and returns one part's arrays. A program takes and returns all parts, laid end to end along the dimension named above; an argument that names none is the same for every part. Nothing has to cross between parts.
Inputs may be any that keep to these rules, and one draw needn't show every extreme that they name: `tile_step`: the 1 local steps of one block row and replica are distinct. `tile_count`: slot 0 of replica 0 is never empty, so every degree is positive.
All inputs are finite; a program needn't handle non-finite values.
Results may differ from the reference program's by a relative error of at most 0.0063.
Values may be sent and summed in bfloat16 or wider, within the bound.
No kernel may reach another device: no remote copies, remote signals or barrier semaphores. Data moves between devices by JAX's collectives and lax.ppermute only.
A program may use at most 64 MiB of HBM per device.

```python
import math
import jax
import jax.numpy as jnp
import numpy as np
from jax import lax

D = 256
FFH = 512
EXPERTS = 8
TILE = 896
HALF = 4
SLOTS = 1
NODES = 7168
N_GRID = 8
N_REP = 2


def draw_tile_step(key, part):
    key = jax.random.fold_in(key, 11)
    keys = jax.random.split(key, N_GRID * N_REP)

    def one_row(row_key):
        return jax.random.permutation(row_key, N_GRID // 2)[:SLOTS]
    steps = jax.vmap(one_row)(keys)
    return steps.reshape(N_GRID, N_REP, SLOTS).astype(jnp.int32)


def draw_tile_count(key, part):
    key = jax.random.fold_in(key, 12)
    first_key, second_key, third_key = jax.random.split(key, 3)
    shape = (N_GRID, N_REP, SLOTS)
    base = jax.random.randint(first_key, shape, 1, 64)
    level = jax.random.randint(second_key, (N_GRID, 1, 1), 0, 3)
    vacant = jax.random.randint(third_key, shape, 0, 4) < level
    row_index = lax.broadcasted_iota(jnp.int32, shape, 0)
    rep_index = lax.broadcasted_iota(jnp.int32, shape, 1)
    slot_index = lax.broadcasted_iota(jnp.int32, shape, 2)
    anchor = (rep_index == 0) & (slot_index == 0)
    counts = jnp.where(vacant & jnp.logical_not(anchor), 0, base)
    counts = jnp.where((row_index == 0) & anchor, 63, counts)
    counts = jnp.where((row_index == 0) & (rep_index == 1) & (slot_index == SLOTS - 1), 0, counts)
    return counts.astype(jnp.int32)


def with_ends(entries, stream_key, least, top_value):
    shape = entries.shape
    place = [jax.random.randint(jax.random.fold_in(stream_key, axis), (), 0, shape[axis]) for axis in range(len(shape))]
    entries = entries.at[tuple(place)].set(least)
    longest = shape.index(max(shape))
    place[longest] = (place[longest] + 1) % shape[longest]
    return entries.at[tuple(place)].set(top_value)


def steps_of(own_key, extent, pieces, smallest, largest):
    level, own = 1.0, jax.random.fold_in(own_key, 6)
    for axis_at, blocks in pieces:
        steps = jnp.exp(jax.random.uniform(jax.random.fold_in(own, axis_at), (blocks,), jnp.float32, smallest / len(pieces), largest / len(pieces)))
        level = level * jnp.repeat(steps, extent[axis_at] // blocks).reshape([-1 if axis == axis_at else 1 for axis in range(len(extent))])
    return level


def rank_table(amount, skew):
    weights = [(1 << 20) // math.isqrt(standing ** skew) + 1 for standing in range(1, amount + 1)]
    spread = 1 + sum(weights) // (1 << 30)
    return np.cumsum(np.array([max(1, weight // spread) for weight in weights]))


def ranked(stream_key, dims, amount, slope):
    listing = rank_table(amount, slope)
    pick = jax.random.randint(jax.random.fold_in(stream_key, 1), dims, 0, int(listing[amount - 1]))
    grade = jnp.searchsorted(jnp.asarray(listing, jnp.int32), pick, side="right")
    return jax.random.permutation(jax.random.fold_in(stream_key, 2), amount)[grade].astype(jnp.int32)


def bell_draw(stream_key, shape, width, reach, cuts=(), kind=jnp.bfloat16):
    factor_of = steps_of(stream_key, shape, cuts, -0.22, 0.18) if cuts else 1.0
    entries = jax.random.normal(stream_key, shape, jnp.float32) * width * factor_of
    return jnp.minimum(jnp.maximum(entries, -reach), reach).astype(kind)


def setup_inputs(seed: int = 0, part: int = 0) -> dict:
    key_of = jax.random.split(jax.random.key(seed), 10)
    part_splits = jax.random.split(jax.random.fold_in(key_of[9], part), 10)
    feats = bell_draw(part_splits[0], (NODES, D), 1.0, 6.0, ((0, 8),))
    msg_weight = bell_draw(key_of[1], (D, D), D ** -0.5, 0.375)
    tiles = bell_draw(part_splits[2], (N_GRID, N_REP, SLOTS, TILE, TILE), TILE ** -0.5, 0.1875, ((0, 8), (1, 2)))
    tile_step = draw_tile_step(jax.random.fold_in(jax.random.fold_in(key_of[9], part), 71), part)
    tile_count = draw_tile_count(jax.random.fold_in(jax.random.fold_in(key_of[9], part), 71), part)
    node_type = with_ends(ranked(part_splits[5], (NODES,), EXPERTS, 2), jax.random.fold_in(part_splits[5], 3), 0, EXPERTS - 1).astype(jnp.int32)
    expert_up = bell_draw(key_of[6], (EXPERTS, D, FFH), D ** -0.5, 0.375)
    expert_down = bell_draw(key_of[7], (EXPERTS, FFH, D), FFH ** -0.5, 0.25)
    out_grad = bell_draw(part_splits[8], (NODES, D), 1.0, 6.0, ((0, 16),))
    return {"feats": feats, "msg_weight": msg_weight, "tiles": tiles, "tile_step": tile_step, "tile_count": tile_count, "node_type": node_type, "expert_up": expert_up, "expert_down": expert_down, "out_grad": out_grad}


def expert_rows(rows, weights, node_type):
    total = jnp.zeros((rows.shape[0], weights.shape[2]), jnp.float32)
    for expert_id in range(EXPERTS):
        product = jnp.dot(rows, weights[expert_id], preferred_element_type=jnp.float32)
        total = total + jnp.where(node_type[:, None] == expert_id, product, jnp.float32(0.0))
    return total

def reference(feats, msg_weight, tiles, tile_step, tile_count, node_type, expert_up, expert_down, out_grad):
    message = jnp.dot(feats, msg_weight, preferred_element_type=jnp.float32).astype(jnp.bfloat16)
    blocks = message.reshape(N_GRID, TILE, D)
    degree = lax.optimization_barrier(jnp.sum(tile_count, axis=(1, 2))).astype(jnp.float32)
    row_ids = jnp.arange(N_GRID, dtype=jnp.int32)[:, None, None]
    rep_ids = jnp.arange(N_REP, dtype=jnp.int32)[None, :, None]
    source = jnp.mod(row_ids - rep_ids * HALF - tile_step, N_GRID).astype(jnp.int32)
    counts = tile_count.astype(jnp.float32)

    def forward_row(inputs):
        tile_row, source_row, count_row = inputs
        holding = blocks[source_row].astype(jnp.float32)
        product = jnp.einsum('rkab,rkbd->rkad', tile_row.astype(jnp.float32), holding)
        return jnp.einsum('rk,rkad->ad', count_row, product)
    sums = lax.map(forward_row, (tiles, source, counts))
    aggregate = (sums / degree[:, None, None]).reshape(N_GRID * TILE, D)
    inv_rms = lax.rsqrt(lax.optimization_barrier(jnp.mean(aggregate * aggregate, axis=-1, keepdims=True)) + 1e-06)
    normed = aggregate * inv_rms
    normed_bf = normed.astype(jnp.bfloat16)
    up_act = expert_rows(normed_bf, expert_up, node_type)
    hidden = jax.nn.silu(up_act).astype(jnp.bfloat16)
    expert_out = expert_rows(hidden, expert_down, node_type)
    updated = (feats.astype(jnp.float32) + expert_out).astype(jnp.bfloat16)
    grad_hidden = expert_rows(out_grad, jnp.swapaxes(expert_down, 1, 2), node_type)
    sigmoid_act = jax.nn.sigmoid(up_act)
    grad_act = (grad_hidden * sigmoid_act * (1.0 + up_act * (1.0 - sigmoid_act))).astype(jnp.bfloat16)
    grad_pre = expert_rows(grad_act, jnp.swapaxes(expert_up, 1, 2), node_type)
    grad_agg = inv_rms * (grad_pre - normed * lax.optimization_barrier(jnp.mean(grad_pre * normed, axis=-1, keepdims=True)))
    grad_scaled = (grad_agg.reshape(N_GRID, TILE, D) / degree[:, None, None]).astype(jnp.bfloat16)

    def backward_row(carry, inputs):
        tile_row, source_row, count_row, grad_row = inputs
        contrib = jnp.einsum('rkba,bd->rkad', tile_row.astype(jnp.float32), grad_row.astype(jnp.float32))
        contrib = contrib * count_row[:, :, None, None]
        return (carry.at[source_row].add(contrib), None)
    start_carry = jnp.zeros((N_GRID, TILE, D), jnp.float32)
    grad_blocks, unused = lax.scan(backward_row, start_carry, (tiles, source, counts, grad_scaled))
    grad_msg = grad_blocks.reshape(N_GRID * TILE, D).astype(jnp.bfloat16)
    feats_grad = (out_grad.astype(jnp.float32) + jnp.dot(grad_msg, msg_weight.T, preferred_element_type=jnp.float32)).astype(jnp.bfloat16)
    msg_weight_grad = jnp.dot(feats.T, grad_msg, preferred_element_type=jnp.float32)
    return (updated, feats_grad, msg_weight_grad)
```

```python
import functools

import jax
import jax.numpy as jnp
from jax import lax
from jax.experimental import pallas as pl
from jax.experimental.pallas import tpu as pltpu
from jax.sharding import PartitionSpec as P

BF16 = jnp.bfloat16
F32 = jnp.float32
NT = (((1,), (1,)), ((), ()))
TN = (((0,), (0,)), ((), ()))
VMEM_LIMIT = 30 * 1024 * 1024


def ring_order(size):
    if size <= 8:
        return list(range(0, size, 2)) + list(range(1, size, 2))[::-1]
    return list(range(size))


def along_ring(block, order, hop):
    size = len(order)
    route = [(order[place], order[(place + hop) % size]) for place in range(size)]
    return lax.ppermute(block, "grid", route)


def other_core(block):
    return lax.ppermute(block, "rep", [(0, 1), (1, 0)])


def call(kernel, out_shape, smem, vmem, scratch=(), flops=0):
    return pl.pallas_call(
        kernel,
        out_shape=out_shape,
        in_specs=[pl.BlockSpec(memory_space=pltpu.SMEM)] * len(smem)
        + [pl.BlockSpec(memory_space=pltpu.VMEM)] * len(vmem),
        out_specs=jax.tree.map(lambda _: pl.BlockSpec(memory_space=pltpu.VMEM), out_shape),
        scratch_shapes=list(scratch),
        compiler_params=pltpu.CompilerParams(vmem_limit_bytes=VMEM_LIMIT),
        cost_estimate=pl.CostEstimate(flops=flops, bytes_accessed=1 << 20, transcendentals=0),
    )(*smem, *vmem)


def struct(shape, dtype):
    return jax.ShapeDtypeStruct(shape, dtype)


def pick_kernel(offsets, slots, parts, *refs):
    weight = refs[parts]
    rows_out, message_out = refs[parts + 1], refs[parts + 2]
    part_offsets, part_rows = offsets
    chosen = refs[0]
    blocks = refs[1:parts]
    for slot in range(slots):
        for block, offset, start in zip(blocks, part_offsets, part_rows, strict=True):

            @pl.when(chosen[slot] == offset)
            def _(slot=slot, block=block, start=start):
                rows_out[slot, pl.ds(start, block.shape[0]), :] = block[...]

        message_out[slot] = jnp.dot(
            rows_out[slot], weight[...], preferred_element_type=F32
        ).astype(BF16)


def hidden_grad_kernel(mask, out_grad, down, grad_hidden):
    experts = down.shape[0]
    total = lax.dot_general(out_grad[...] * mask[0], down[0], NT, preferred_element_type=F32)
    for expert in range(1, experts):
        total += lax.dot_general(
            out_grad[...] * mask[expert], down[expert], NT, preferred_element_type=F32
        )
    grad_hidden[...] = total


def middle_kernel(
    place,
    counts,
    own_rows,
    other_rows,
    own_message,
    other_message,
    mask,
    up,
    grad_hidden,
    hidden,
    grad_scaled,
    message,
    wide,
):
    slots = own_rows.shape[0]
    experts, width, inner = up.shape
    half = own_message.shape[1]
    core = place[0]
    own_start = pl.multiple_of(core * half, half)
    other_start = pl.multiple_of((1 - core) * half, half)
    for slot in range(2 * slots):
        message[slot, pl.ds(own_start, half), :] = own_message[slot]
        message[slot, pl.ds(other_start, half), :] = other_message[slot]
    total = jnp.zeros((half, width), F32)
    edges = jnp.float32(0.0)
    for slot in range(slots):
        for tile_rows, which in ((own_rows, core), (other_rows, 1 - core)):
            index = which * slots + slot
            count = counts[index].astype(F32)
            edges = edges + count
            total += count * jnp.dot(tile_rows[slot], message[index], preferred_element_type=F32)
    aggregate = total / jnp.full((1, 1), edges, F32)
    inv_rms = lax.rsqrt(jnp.mean(aggregate * aggregate, axis=-1, keepdims=True) + 1e-06)
    normed = aggregate * inv_rms
    normed_bf = normed.astype(BF16)
    for expert in range(experts):
        wide[:, expert * width : (expert + 1) * width] = normed_bf * mask[expert]
    up_act = jnp.dot(
        wide[...], up[...].reshape(experts * width, inner), preferred_element_type=F32
    )
    gate = 1.0 / (1.0 + jnp.exp(-up_act))
    hidden[...] = (up_act * gate).astype(BF16)
    grad_act = (grad_hidden[...] * gate * (1.0 + up_act * (1.0 - gate))).astype(BF16)
    grad_pre = jnp.zeros((half, width), F32)
    for expert in range(experts):
        masked = jnp.concatenate(
            [
                grad_act[:, start : start + width] * mask[expert]
                for start in range(0, inner, width)
            ],
            axis=1,
        )
        grad_pre += lax.dot_general(masked, up[expert], NT, preferred_element_type=F32)
    grad_agg = inv_rms * (
        grad_pre - normed * jnp.mean(grad_pre * normed, axis=-1, keepdims=True)
    )
    grad_scaled[...] = (grad_agg / jnp.full((1, 1), edges, F32)).astype(BF16)


def spread_kernel(
    offsets, place, counts, chosen, own_columns, other_columns, own_grad, other_grad, *refs
):
    terms, grads, full_grad = refs[:-2], refs[-2], refs[-1]
    slots, half, _ = own_columns.shape
    core = place[0]
    full_grad[pl.ds(pl.multiple_of(core * half, half), half), :] = own_grad[...]
    full_grad[pl.ds(pl.multiple_of((1 - core) * half, half), half), :] = other_grad[...]
    products, distances = [], []
    for columns, which in ((own_columns, core), (other_columns, 1 - core)):
        for slot in range(slots):
            index = which * slots + slot
            product = counts[index].astype(F32) * jnp.dot(
                columns[slot], full_grad[...], preferred_element_type=F32
            )
            grads[index] = product.astype(BF16)
            products.append(product)
            distances.append(chosen[index])
    for term, (offset, start) in zip(terms, offsets, strict=True):
        length = term.shape[0]
        total = None
        for product, distance in zip(products, distances, strict=True):
            piece = jnp.where(distance == offset, product[start : start + length], 0.0)
            total = piece if total is None else total + piece
        term[...] = total.astype(term.dtype)


def weight_kernel(rows, grads, total):
    slots = rows.shape[0]
    total[...] = sum(
        lax.dot_general(rows[slot], grads[slot], TN, preferred_element_type=F32)
        for slot in range(slots)
    )


def update_kernel(mask, hidden, down, feats, updated):
    experts, inner, width = down.shape
    total = feats[...].astype(F32)
    for expert in range(experts):
        masked = jnp.concatenate(
            [
                hidden[:, start : start + width] * mask[expert]
                for start in range(0, inner, width)
            ],
            axis=1,
        )
        total += jnp.dot(masked, down[expert], preferred_element_type=F32)
    updated[...] = total.astype(BF16)


def finish_kernel(own, up_first, up_second, down_first, down_second, weight, out_grad, result):
    cut = up_first.shape[0]
    for start, pair in ((0, (up_first, down_first)), (cut, (up_second, down_second))):
        length = pair[0].shape[0]
        grad_msg = (
            own[start : start + length] + pair[0][...].astype(F32) + pair[1][...].astype(F32)
        ).astype(BF16)
        back = lax.dot_general(grad_msg, weight[...], NT, preferred_element_type=F32)
        result[start : start + length] = (
            out_grad[start : start + length].astype(F32) + back
        ).astype(BF16)


def sum_over_all(term, size, core):
    half = term.shape[0] // 2
    kept = lax.dynamic_slice_in_dim(term, core * half, half, 0)
    total = kept + other_core(lax.dynamic_slice_in_dim(term, (1 - core) * half, half, 0))
    step = 1
    while step < size:
        total = total + lax.ppermute(total, "grid", [(i, i ^ step) for i in range(size)])
        step *= 2
    received = other_core(total)
    first = jnp.where(core == 0, total, received)
    second = jnp.where(core == 0, received, total)
    return jnp.concatenate([first, second], axis=0)


def per_device(
    feats, msg_weight, tiles, tile_step, tile_count, node_type, expert_up, expert_down, out_grad
):
    size = lax.axis_size("grid")
    core = lax.axis_index("rep")
    chip = lax.axis_index("grid")
    order = ring_order(size)
    far = size // 2
    slots = tiles.shape[2]
    block, width = feats.shape
    half = block // 2
    cut = half // 2
    experts, _, inner = expert_up.shape

    first = lax.dynamic_slice_in_dim(feats, core * half, cut, 0)
    second = lax.dynamic_slice_in_dim(feats, core * half + cut, half - cut, 0)
    arrived = [(0, 0, first), (0, cut, second)]
    up_a = down_a = first
    up_b = down_b = second
    for step in range(1, far):
        up_a = along_ring(up_a, order, 1)
        down_b = along_ring(down_b, order, -1)
        up_b = along_ring(up_b, order, 1)
        down_a = along_ring(down_a, order, -1)
        arrived += [(size - step, 0, up_a), (size - step, cut, up_b)]
        arrived += [(step, 0, down_a), (step, cut, down_b)]
    arrived += [(far, 0, along_ring(up_a, order, 1)), (far, cut, along_ring(down_b, order, -1))]

    tile_own = tiles[0, 0]
    table_own = jnp.stack([tile_step[0, 0], tile_count[0, 0]])
    table_other = other_core(table_own)
    tile_other = other_core(tile_own)
    table = jnp.where(
        core == 0, jnp.stack([table_own, table_other]), jnp.stack([table_other, table_own])
    )
    counts = table[:, 1].reshape(2 * slots)
    half_loop = jnp.arange(2, dtype=jnp.int32)[:, None] * far
    source = jnp.mod(chip - half_loop - table[:, 0], size)
    ring_place = jnp.array([order.index(i) for i in range(size)], jnp.int32)
    distance = jnp.mod(ring_place[source] - ring_place[chip], size).reshape(2 * slots)
    place = core.astype(jnp.int32).reshape(1)

    def rows_of(tile):
        return lax.dynamic_slice_in_dim(tile, core * half, half, 1)

    def columns_of(tile):
        return lax.dynamic_slice_in_dim(jnp.swapaxes(tile, 1, 2), core * half, half, 1)

    types = lax.dynamic_slice_in_dim(node_type, core * half, half, 0)
    mask = (types[None, :] == jnp.arange(experts, dtype=jnp.int32)[:, None]).astype(BF16)
    mask = jnp.broadcast_to(mask[:, :, None], (experts, half, width))
    grad_hidden = call(
        hidden_grad_kernel, struct((half, inner), F32), (), (mask, out_grad, expert_down)
    )

    pieces = [piece for _, _, piece in arrived]
    offsets = ([offset for offset, _, _ in arrived], [start for _, start, _ in arrived])
    source_rows, own_message = call(
        functools.partial(pick_kernel, offsets, 2 * slots, len(pieces) + 1),
        [struct((2 * slots, half, width), BF16)] * 2,
        (distance,),
        (*pieces, msg_weight),
    )
    other_message = other_core(own_message)

    hidden, grad_scaled = call(
        middle_kernel,
        [struct((half, inner), BF16), struct((half, width), BF16)],
        (place, counts),
        (
            rows_of(tile_own),
            rows_of(tile_other),
            own_message,
            other_message,
            mask,
            expert_up,
            grad_hidden,
        ),
        (
            pltpu.VMEM((2 * slots, block, width), BF16),
            pltpu.VMEM((half, experts * width), BF16),
        ),
    )
    other_grad = other_core(grad_scaled)

    keys = [(0, 0), (far, 0), (far, cut)]
    shapes = [struct((half, width), F32), struct((cut, width), BF16)]
    shapes += [struct((half - cut, width), BF16)]
    for step in range(1, far):
        for offset in (step, size - step):
            keys += [(offset, 0), (offset, cut)]
            shapes += [struct((cut, width), BF16), struct((half - cut, width), BF16)]
    *terms, grads = call(
        functools.partial(spread_kernel, keys),
        [*shapes, struct((2 * slots, half, width), BF16)],
        (place, counts, distance),
        (columns_of(tile_own), columns_of(tile_other), grad_scaled, other_grad),
        (pltpu.VMEM((block, width), BF16),),
    )
    terms = dict(zip(keys, terms, strict=True))

    def joined(received, term):
        return (received.astype(F32) + term.astype(F32)).astype(BF16)

    up_a = along_ring(terms[far, 0], order, 1)
    down_b = along_ring(terms[far, cut], order, -1)
    up_b = down_a = None
    for step in range(far - 1, 0, -1):
        up_a = along_ring(joined(up_a, terms[step, 0]), order, 1)
        down_b = along_ring(joined(down_b, terms[size - step, cut]), order, -1)
        ready_b, ready_a = terms[step, cut], terms[size - step, 0]
        up_b = along_ring(ready_b if up_b is None else joined(up_b, ready_b), order, 1)
        down_a = along_ring(ready_a if down_a is None else joined(down_a, ready_a), order, -1)

    weight_term = call(
        weight_kernel, struct((width, width), F32), (), (source_rows, grads)
    )
    msg_weight_grad = sum_over_all(weight_term, size, core)

    own_feats = jnp.concatenate([first, second], axis=0)
    updated = call(
        update_kernel,
        struct((half, width), BF16),
        (),
        (mask, hidden, expert_down, own_feats),
    )
    feats_grad = call(
        finish_kernel,
        struct((half, width), BF16),
        (),
        (terms[0, 0], up_a, up_b, down_a, down_b, msg_weight, out_grad),
    )
    return (updated, feats_grad, msg_weight_grad)


def solution(mesh):
    return jax.shard_map(
        per_device,
        mesh=mesh,
        in_specs=(
            P(("groups", "grid"), None),
            P(),
            P(("groups", "grid"), "rep", None, None, None),
            P(("groups", "grid"), "rep", None),
            P(("groups", "grid"), "rep", None),
            P(("groups", "grid")),
            P(),
            P(),
            P(("groups", "grid", "rep"), None),
        ),
        out_specs=(
            P(("groups", "grid", "rep"), None),
            P(("groups", "grid", "rep"), None),
            P("groups", None),
        ),
        check_vma=False,
    )
```

```python
import functools

import jax
import jax.numpy as jnp
from jax import lax
from jax.experimental import pallas as pl
from jax.experimental.pallas import tpu as pltpu
from jax.sharding import PartitionSpec as P

BF16 = jnp.bfloat16
F32 = jnp.float32
NT = (((1,), (1,)), ((), ()))
TN = (((0,), (0,)), ((), ()))
VMEM_LIMIT = 30 * 1024 * 1024


def ring_order(size):
    if size <= 8:
        return list(range(0, size, 2)) + list(range(1, size, 2))[::-1]
    return list(range(size))


def along_ring(block, order, hop):
    size = len(order)
    route = [(order[place], order[(place + hop) % size]) for place in range(size)]
    return lax.ppermute(block, "grid", route)


def other_core(block):
    return lax.ppermute(block, "rep", [(0, 1), (1, 0)])


def swapped(block, distance, across=False):
    axes, flip = ("grid", "rep"), 2 * distance + int(across)
    route = [(device, device ^ flip) for device in range(2 * lax.axis_size("grid"))]
    return lax.ppermute(block, axes, route)


def call(kernel, out_shape, smem, vmem, scratch=(), flops=0):
    moved = sum(item.size * item.dtype.itemsize for item in (*vmem, *jax.tree.leaves(out_shape)))
    return pl.pallas_call(
        kernel,
        out_shape=out_shape,
        in_specs=[pl.BlockSpec(memory_space=pltpu.SMEM)] * len(smem)
        + [pl.BlockSpec(memory_space=pltpu.VMEM)] * len(vmem),
        out_specs=jax.tree.map(lambda _: pl.BlockSpec(memory_space=pltpu.VMEM), out_shape),
        scratch_shapes=list(scratch),
        compiler_params=pltpu.CompilerParams(vmem_limit_bytes=VMEM_LIMIT),
        cost_estimate=pl.CostEstimate(flops=flops, bytes_accessed=moved, transcendentals=0),
    )(*smem, *vmem)


def struct(shape, dtype):
    return jax.ShapeDtypeStruct(shape, dtype)


def ring_place(chip, size):
    if size <= 8:
        return jnp.where(lax.rem(chip, 2) == 0, lax.div(chip, 2), size - 1 - lax.div(chip, 2))
    return chip


def distances(place, own_table, other_table, size):
    core, chip = place[0], place[1]
    slots = own_table.shape[1]
    found = []
    for replica in range(2):
        for slot in range(slots):
            step = jnp.where(core == replica, own_table[0, slot], other_table[0, slot])
            source = lax.rem(chip - replica * (size // 2) - step + 2 * size, size)
            found.append(lax.rem(ring_place(source, size) - ring_place(chip, size) + size, size))
    return found


def edge_counts(place, own_table, other_table):
    core = place[0]
    slots = own_table.shape[1]
    return [
        jnp.where(core == replica, own_table[1, slot], other_table[1, slot]).astype(F32)
        for replica in range(2)
        for slot in range(slots)
    ]


def flip_kernel(tile, flipped):
    for slot in range(tile.shape[0]):
        flipped[slot] = jnp.swapaxes(tile[slot], 0, 1)


def pick_kernel(size, offsets, place, own_table, other_table, *refs):
    blocks, rows = refs[:-1], refs[-1]
    chosen = distances(place, own_table, other_table, size)
    for slot in range(rows.shape[0]):
        for block, (offset, start) in zip(blocks, offsets, strict=True):

            @pl.when(chosen[slot] == offset)
            def _(slot=slot, block=block, start=start):
                rows[slot, pl.ds(start, block.shape[0]), :] = block[...]


def prepare_kernel(place, types, out_grad, down, mask, grad_hidden, column):
    experts, half, width = mask.shape
    block = types.shape[0]
    row = types[...].astype(F32).reshape(1, block)
    column[...] = jnp.swapaxes(jnp.broadcast_to(row, (8, block)), 0, 1)
    own = column[pl.ds(pl.multiple_of(place[0] * half, half), half), 0:1]
    own = jnp.broadcast_to(own, (half, width))
    total = None
    for expert in range(experts):
        mask[expert] = jnp.where(own == expert, 1.0, 0.0).astype(BF16)
        term = lax.dot_general(
            out_grad[...] * mask[expert], down[expert], NT, preferred_element_type=F32
        )
        total = term if total is None else total + term
    grad_hidden[...] = total


def middle_kernel(
    place,
    own_table,
    other_table,
    own_tile,
    other_tile,
    own_rows,
    other_rows,
    weight,
    mask,
    up,
    grad_hidden,
    hidden,
    packed,
    kept,
    rows,
    wide,
):
    slots = own_tile.shape[0]
    experts, width, inner = up.shape
    half = own_rows.shape[1]
    core = place[0]
    own_start = pl.multiple_of(core * half, half)
    other_start = pl.multiple_of((1 - core) * half, half)
    for slot in range(2 * slots):
        rows[slot, pl.ds(own_start, half), :] = own_rows[slot]
        rows[slot, pl.ds(other_start, half), :] = other_rows[slot]
    total = jnp.zeros((half, width), F32)
    for slot in range(slots):
        for tile, table, which in (
            (own_tile, own_table, core),
            (other_tile, other_table, 1 - core),
        ):
            total += table[1, slot].astype(F32) * jnp.dot(
                tile[slot, pl.ds(own_start, half), :],
                rows[which * slots + slot],
                preferred_element_type=F32,
            )
    high = total.astype(BF16)
    rest = (total - high.astype(F32)).astype(BF16)
    aggregate = jnp.dot(high, weight[...], preferred_element_type=F32)
    aggregate += jnp.dot(rest, weight[...], preferred_element_type=F32)
    edges = jnp.full((1, 1), sum(edge_counts(place, own_table, other_table)), F32)
    aggregate = aggregate / edges
    inv_rms = lax.rsqrt(jnp.mean(aggregate * aggregate, axis=-1, keepdims=True) + 1e-06)
    normed = aggregate * inv_rms
    normed_bf = normed.astype(BF16)
    for expert in range(experts):
        wide[:, expert * width : (expert + 1) * width] = normed_bf * mask[expert]
    up_act = jnp.dot(
        wide[...], up[...].reshape(experts * width, inner), preferred_element_type=F32
    )
    gate = 1.0 / (1.0 + jnp.exp(-up_act))
    hidden[...] = (up_act * gate).astype(BF16)
    grad_act = (grad_hidden[...] * gate * (1.0 + up_act * (1.0 - gate))).astype(BF16)
    grad_pre = jnp.zeros((half, width), F32)
    for expert in range(experts):
        term = lax.dot_general(grad_act, up[expert], NT, preferred_element_type=F32)
        grad_pre += term * mask[expert].astype(F32)
    grad_agg = inv_rms * (
        grad_pre - normed * jnp.mean(grad_pre * normed, axis=-1, keepdims=True)
    )
    grad_scaled = (grad_agg / edges).astype(BF16)
    packed[:half] = grad_scaled
    term = lax.dot_general(high, grad_scaled, TN, preferred_element_type=F32)
    upper, lower = term[: width // 2], term[width // 2 :]
    kept[...] = jnp.where(core == 0, upper, lower)
    packed[half:] = jnp.where(core == 0, lower, upper).astype(BF16)


def product_kernel(
    size,
    place,
    own_table,
    other_table,
    own_flipped,
    other_flipped,
    own_packed,
    other_packed,
    kept,
    products,
    far_first,
    far_second,
    weight_part,
    full_grad,
):
    slots, half = own_flipped.shape[0], products.shape[1]
    core = place[0]
    own_start = pl.multiple_of(core * half, half)
    full_grad[pl.ds(own_start, half), :] = own_packed[:half]
    full_grad[pl.ds(pl.multiple_of((1 - core) * half, half), half), :] = other_packed[:half]
    weight_part[...] = (kept[...] + other_packed[half:].astype(F32)).astype(BF16)
    chosen = distances(place, own_table, other_table, size)
    total = jnp.zeros(products.shape[1:], F32)
    for flipped, table, which in (
        (own_flipped, own_table, core),
        (other_flipped, other_table, 1 - core),
    ):
        for slot in range(slots):
            product = table[1, slot].astype(F32) * jnp.dot(
                flipped[slot, pl.ds(own_start, half), :],
                full_grad[...],
                preferred_element_type=F32,
            )
            products[which * slots + slot] = product
            distance = jnp.where(which == 0, chosen[slot], chosen[slots + slot])
            total += jnp.where(distance == size // 2, product, 0.0)
    cut = far_first.shape[0]
    far_first[...] = total[:cut].astype(BF16)
    far_second[...] = total[cut:].astype(BF16)


def spread_kernel(size, offsets, place, own_table, other_table, products, *terms):
    chosen = distances(place, own_table, other_table, size)
    for term, (offset, start) in zip(terms, offsets, strict=True):
        length = term.shape[0]
        total = jnp.where(chosen[0] == offset, products[0, start : start + length], 0.0)
        for slot in range(1, products.shape[0]):
            total += jnp.where(chosen[slot] == offset, products[slot, start : start + length], 0.0)
        term[...] = total.astype(term.dtype)


def update_kernel(mask, hidden, down, feats_first, feats_second, updated):
    experts, inner, width = down.shape
    total = jnp.concatenate([feats_first[...], feats_second[...]], axis=0).astype(F32)
    for expert in range(experts):
        masked = jnp.concatenate(
            [
                hidden[:, start : start + width] * mask[expert]
                for start in range(0, inner, width)
            ],
            axis=1,
        )
        total += jnp.dot(masked, down[expert], preferred_element_type=F32)
    updated[...] = total.astype(BF16)


def finish_kernel(
    place,
    own,
    up_first,
    up_second,
    down_first,
    down_second,
    weight,
    out_grad,
    own_part,
    own_swapped,
    other_part,
    other_swapped,
    result,
    weight_grad,
):
    cut = up_first.shape[0]
    for start, pair in ((0, (up_first, down_first)), (cut, (up_second, down_second))):
        length = pair[0].shape[0]
        grad_msg = (
            own[start : start + length] + pair[0][...].astype(F32) + pair[1][...].astype(F32)
        ).astype(BF16)
        back = lax.dot_general(grad_msg, weight[...], NT, preferred_element_type=F32)
        result[start : start + length] = (
            out_grad[start : start + length].astype(F32) + back
        ).astype(BF16)
    half = own_part.shape[0]
    upper = own_part[...].astype(F32) + own_swapped[...].astype(F32)
    lower = other_part[...].astype(F32) + other_swapped[...].astype(F32)
    weight_grad[:half] = jnp.where(place[0] == 0, upper, lower)
    weight_grad[half:] = jnp.where(place[0] == 0, lower, upper)


def per_device(
    feats, msg_weight, tiles, tile_step, tile_count, node_type, expert_up, expert_down, out_grad
):
    size = lax.axis_size("grid")
    core = lax.axis_index("rep")
    chip = lax.axis_index("grid")
    order = ring_order(size)
    far = size // 2
    slots = tiles.shape[2]
    block, width = feats.shape
    half = block // 2
    cut = half // 2
    experts, _, inner = expert_up.shape

    first = lax.dynamic_slice_in_dim(feats, core * half, cut, 0)
    second = lax.dynamic_slice_in_dim(feats, core * half + cut, half - cut, 0)

    place = jnp.stack([core, chip]).astype(jnp.int32)
    tile_own, _ = lax.optimization_barrier((tiles[0, 0], first))
    own_table = jnp.stack([tile_step[0, 0], tile_count[0, 0]])
    other_table = other_core(own_table)
    tile_other = other_core(tile_own)
    flip = functools.partial(call, flip_kernel, struct(tile_own.shape, BF16), ())

    arrived = [(0, 0, first), (0, cut, second)]
    up_a = down_a = first
    up_b = down_b = second
    flipped_own = flip((tile_own,))
    for step in range(1, far):
        if step == 2:
            grads_out, _, _ = lax.optimization_barrier((out_grad, up_a, down_b))
            mask, grad_hidden = call(
                prepare_kernel,
                [struct((experts, half, width), BF16), struct((half, inner), F32)],
                (place,),
                (node_type, grads_out, expert_down),
                (pltpu.VMEM((block, 8), F32),),
            )
            up_a, down_b, flipped_own, other_table = lax.optimization_barrier(
                (up_a, down_b, flipped_own, other_table)
            )
        if step == 3:
            up_a, down_b, grad_hidden, mask = lax.optimization_barrier(
                (up_a, down_b, grad_hidden, mask)
            )
        up_a = along_ring(up_a, order, 1)
        down_b = along_ring(down_b, order, -1)
        up_b = along_ring(up_b, order, 1)
        down_a = along_ring(down_a, order, -1)
        arrived += [(size - step, 0, up_a), (size - step, cut, up_b)]
        arrived += [(step, 0, down_a), (step, cut, down_b)]
    tables = (place, own_table, other_table)
    far_first, far_second = along_ring(up_a, order, 1), along_ring(down_b, order, -1)
    arrived += [(far, 0, far_first), (far, cut, far_second)]
    tile_late, _, _ = lax.optimization_barrier((tile_other, up_a, down_b))
    flipped_other = flip((tile_late,))
    source_rows = call(
        functools.partial(pick_kernel, size, [item[:2] for item in arrived]),
        struct((2 * slots, half, width), BF16),
        tables,
        [piece for _, _, piece in arrived],
    )
    other_rows = other_core(source_rows)

    hidden, packed, kept = call(
        middle_kernel,
        [
            struct((half, inner), BF16),
            struct((half + width // 2, width), BF16),
            struct((width // 2, width), F32),
        ],
        tables,
        (
            tile_own,
            tile_other,
            source_rows,
            other_rows,
            msg_weight,
            mask,
            expert_up,
            grad_hidden,
        ),
        (
            pltpu.VMEM((2 * slots, block, width), BF16),
            pltpu.VMEM((half, experts * width), BF16),
        ),
        flops=4 * half * width * (slots * block + experts * inner),
    )
    other_packed = other_core(packed)

    halves = [struct((cut, width), BF16), struct((half - cut, width), BF16)]
    products, up_a, down_b, mine = call(
        functools.partial(product_kernel, size),
        [struct((2 * slots, half, width), F32), *halves, struct((width // 2, width), BF16)],
        tables,
        (flipped_own, flipped_other, packed, other_packed, kept),
        (pltpu.VMEM((block, width), BF16),),
        flops=4 * half * width * slots * block,
    )
    up_a = along_ring(up_a, order, 1)
    down_b = along_ring(down_b, order, -1)
    keys, shapes = [(0, 0)], [struct((half, width), F32)]
    for step in range(far - 1, 0, -1):
        for offset in (step, size - step):
            keys += [(offset, 0), (offset, cut)]
            shapes += halves
    terms = call(functools.partial(spread_kernel, size, keys), shapes, tables, (products,))
    terms = dict(zip(keys, terms, strict=True))

    def joined(received, term):
        return (received.astype(F32) + term.astype(F32)).astype(BF16)

    swap = size // 2
    theirs = swapped(mine, swap)
    up_b, down_a = lax.optimization_barrier(
        (terms[far - 1, cut], terms[size - far + 1, 0], up_a, down_b)
    )[:2]
    for step in range(far - 1, 0, -1):
        up_a = joined(up_a, terms[step, 0])
        down_b = joined(down_b, terms[size - step, cut])
        if step < far - 1:
            up_b = joined(up_b, terms[step, cut])
            down_a = joined(down_a, terms[size - step, 0])
            if swap > 2:
                swap //= 2
                mine = lax.optimization_barrier((joined(mine, theirs), up_a, down_b))[0]
                theirs = swapped(mine, swap)
        if step == 1:
            while swap > 2:
                swap //= 2
                mine = joined(mine, theirs)
                theirs = swapped(mine, swap)
            if swap > 1:
                mine = lax.optimization_barrier((joined(mine, theirs), up_a, down_b))[0]
            weight_parts = (mine, swapped(mine, 1), other_core(mine), swapped(mine, 1, across=True))
        up_a = along_ring(up_a, order, 1)
        down_b = along_ring(down_b, order, -1)
        up_b = along_ring(up_b, order, 1)
        down_a = along_ring(down_a, order, -1)

    updated = call(
        update_kernel,
        struct((half, width), BF16),
        (),
        (mask, hidden, expert_down, first, second),
    )
    feats_grad, msg_weight_grad = call(
        finish_kernel,
        [struct((half, width), BF16), struct((width, width), F32)],
        (place,),
        (
            terms[0, 0],
            up_a,
            up_b,
            down_a,
            down_b,
            msg_weight,
            out_grad,
            *weight_parts,
        ),
    )
    return (updated, feats_grad, msg_weight_grad)


def solution(mesh):
    return jax.shard_map(
        per_device,
        mesh=mesh,
        in_specs=(
            P(("groups", "grid"), None),
            P(),
            P(("groups", "grid"), "rep", None, None, None),
            P(("groups", "grid"), "rep", None),
            P(("groups", "grid"), "rep", None),
            P(("groups", "grid")),
            P(),
            P(),
            P(("groups", "grid", "rep"), None),
        ),
        out_specs=(
            P(("groups", "grid", "rep"), None),
            P(("groups", "grid", "rep"), None),
            P("groups", None),
        ),
        check_vma=False,
    )
```

```python
import functools
import math

import jax
import jax.numpy as jnp
from jax import lax
from jax.experimental import pallas as pl
from jax.experimental.pallas import tpu as pltpu
from jax.sharding import PartitionSpec as P

BF16 = jnp.bfloat16
F32 = jnp.float32
NT = (((1,), (1,)), ((), ()))
TN = (((0,), (0,)), ((), ()))
SPARE_VMEM = 8 * 1024 * 1024


def ring_order(size):
    if size <= 8:
        return list(range(0, size, 2)) + list(range(1, size, 2))[::-1]
    return list(range(size))


def along_ring(block, order, hop):
    size = len(order)
    route = [(order[place], order[(place + hop) % size]) for place in range(size)]
    return lax.ppermute(block, "grid", route)


def other_core(block):
    return lax.ppermute(block, "rep", [(0, 1), (1, 0)])


def swapped(block, distance, across=False):
    axes, flip = ("grid", "rep"), 2 * distance + int(across)
    route = [(device, device ^ flip) for device in range(2 * lax.axis_size("grid"))]
    return lax.ppermute(block, axes, route)


def call(kernel, out_shape, smem, vmem, scratch=(), flops=0, space=pltpu.VMEM):
    held = (*vmem, *jax.tree.leaves(out_shape))
    moved = sum(math.prod(item.shape) * item.dtype.itemsize for item in held)
    spare = sum(math.prod(item.shape) * 4 for item in scratch) + SPARE_VMEM
    return pl.pallas_call(
        kernel,
        out_shape=out_shape,
        in_specs=[pl.BlockSpec(memory_space=pltpu.SMEM)] * len(smem)
        + [pl.BlockSpec(memory_space=space)] * len(vmem),
        out_specs=jax.tree.map(lambda _: pl.BlockSpec(memory_space=pltpu.VMEM), out_shape),
        scratch_shapes=list(scratch),
        compiler_params=pltpu.CompilerParams(vmem_limit_bytes=moved + spare),
        cost_estimate=pl.CostEstimate(flops=flops, bytes_accessed=moved, transcendentals=0),
    )(*smem, *vmem)


def struct(shape, dtype):
    return jax.ShapeDtypeStruct(shape, dtype)


def ring_place(chip, size):
    if size <= 8:
        return jnp.where(lax.rem(chip, 2) == 0, lax.div(chip, 2), size - 1 - lax.div(chip, 2))
    return chip


def distances(place, own_table, other_table, size):
    core, chip = place[0], place[1]
    slots = own_table.shape[1]
    found = []
    for replica in range(2):
        for slot in range(slots):
            step = jnp.where(core == replica, own_table[0, slot], other_table[0, slot])
            source = lax.rem(chip - replica * (size // 2) - step + 2 * size, size)
            found.append(lax.rem(ring_place(source, size) - ring_place(chip, size) + size, size))
    return found


def edge_counts(place, own_table, other_table):
    core = place[0]
    slots = own_table.shape[1]
    return [
        jnp.where(core == replica, own_table[1, slot], other_table[1, slot]).astype(F32)
        for replica in range(2)
        for slot in range(slots)
    ]


def flip_kernel(tile, flipped):
    for slot in range(tile.shape[0]):
        flipped[slot] = jnp.swapaxes(tile[slot], 0, 1)


def pick_kernel(size, offsets, place, own_table, other_table, *refs):
    blocks, rows = refs[:-1], refs[-1]
    chosen = distances(place, own_table, other_table, size)
    for slot in range(rows.shape[0]):
        for block, (offset, start) in zip(blocks, offsets, strict=True):

            @pl.when(chosen[slot] == offset)
            def _(slot=slot, block=block, start=start):
                rows[slot, pl.ds(start, block.shape[0]), :] = block[...]


def prepare_kernel(place, types, out_grad, down, mask, grad_hidden, column):
    experts, half, width = mask.shape
    block = types.shape[0]
    row = types[...].astype(F32).reshape(1, block)
    column[...] = jnp.swapaxes(jnp.broadcast_to(row, (8, block)), 0, 1)
    own = column[pl.ds(pl.multiple_of(place[0] * half, half), half), 0:1]
    own = jnp.broadcast_to(own, (half, width))
    total = None
    for expert in range(experts):
        mask[expert] = jnp.where(own == expert, 1.0, 0.0).astype(BF16)
        term = lax.dot_general(
            out_grad[...] * mask[expert], down[expert], NT, preferred_element_type=F32
        )
        total = term if total is None else total + term
    grad_hidden[...] = total


def middle_kernel(
    place,
    own_table,
    other_table,
    own_tile,
    other_tile,
    own_rows,
    other_rows,
    weight,
    mask,
    up,
    grad_hidden,
    hidden,
    packed,
    kept,
    rows,
    wide,
):
    slots = own_tile.shape[0]
    experts, width, inner = up.shape
    half = own_rows.shape[1]
    core = place[0]
    own_start = pl.multiple_of(core * half, half)
    other_start = pl.multiple_of((1 - core) * half, half)
    for slot in range(2 * slots):
        rows[slot, pl.ds(own_start, half), :] = own_rows[slot]
        rows[slot, pl.ds(other_start, half), :] = other_rows[slot]
    total = jnp.zeros((half, width), F32)
    for slot in range(slots):
        for tile, table, which in (
            (own_tile, own_table, core),
            (other_tile, other_table, 1 - core),
        ):
            total += table[1, slot].astype(F32) * jnp.dot(
                tile[slot, pl.ds(own_start, half), :],
                rows[which * slots + slot],
                preferred_element_type=F32,
            )
    high = total.astype(BF16)
    rest = (total - high.astype(F32)).astype(BF16)
    aggregate = jnp.dot(high, weight[...], preferred_element_type=F32)
    aggregate += jnp.dot(rest, weight[...], preferred_element_type=F32)
    edges = jnp.full((1, 1), sum(edge_counts(place, own_table, other_table)), F32)
    aggregate = aggregate / edges
    inv_rms = lax.rsqrt(jnp.mean(aggregate * aggregate, axis=-1, keepdims=True) + 1e-06)
    normed = aggregate * inv_rms
    normed_bf = normed.astype(BF16)
    for expert in range(experts):
        wide[:, expert * width : (expert + 1) * width] = normed_bf * mask[expert]
    up_act = jnp.dot(
        wide[...], up[...].reshape(experts * width, inner), preferred_element_type=F32
    )
    gate = 1.0 / (1.0 + jnp.exp(-up_act))
    hidden[...] = (up_act * gate).astype(BF16)
    grad_act = (grad_hidden[...] * gate * (1.0 + up_act * (1.0 - gate))).astype(BF16)
    grad_pre = jnp.zeros((half, width), F32)
    for expert in range(experts):
        term = lax.dot_general(grad_act, up[expert], NT, preferred_element_type=F32)
        grad_pre += term * mask[expert].astype(F32)
    grad_agg = inv_rms * (
        grad_pre - normed * jnp.mean(grad_pre * normed, axis=-1, keepdims=True)
    )
    grad_scaled = (grad_agg / edges).astype(BF16)
    packed[:half] = grad_scaled
    term = lax.dot_general(high, grad_scaled, TN, preferred_element_type=F32)
    upper, lower = term[: width // 2], term[width // 2 :]
    kept[...] = jnp.where(core == 0, upper, lower)
    sent = jnp.where(core == 0, lower, upper)
    packed[half : half + width // 2] = sent.astype(BF16)
    packed[half + width // 2 :] = (sent - sent.astype(BF16).astype(F32)).astype(BF16)


def product_kernel(
    size,
    offsets,
    place,
    own_table,
    other_table,
    own_flipped,
    other_flipped,
    own_packed,
    other_packed,
    kept,
    products,
    far_first,
    far_second,
    weight_part,
    *rest,
):
    terms, full_grad = rest[:-1], rest[-1]
    slots, half = own_flipped.shape[0], products.shape[1]
    core = place[0]
    own = pl.ds(pl.multiple_of(core * half, half), half)
    full_grad[own, :] = own_packed[:half]
    full_grad[pl.ds(pl.multiple_of((1 - core) * half, half), half), :] = other_packed[:half]
    middle = half + kept.shape[0]
    weight_part[...] = (
        kept[...] + other_packed[half:middle].astype(F32) + other_packed[middle:].astype(F32)
    ).astype(BF16)
    for flipped, table, which in (
        (own_flipped, own_table, core),
        (other_flipped, other_table, 1 - core),
    ):
        for slot in range(slots):
            products[which * slots + slot] = table[1, slot].astype(F32) * jnp.dot(
                flipped[slot, own, :], full_grad[...], preferred_element_type=F32
            )
    chosen = distances(place, own_table, other_table, size)
    total = gathered(chosen, products, size // 2)
    cut = far_first.shape[0]
    far_first[...] = total[:cut].astype(BF16)
    far_second[...] = total[cut:].astype(BF16)
    for term, offset in zip(terms, offsets, strict=True):
        term[...] = gathered(chosen, products, offset).astype(BF16)


def gathered(chosen, products, offset):
    total = jnp.where(chosen[0] == offset, products[0], 0.0)
    for slot in range(1, products.shape[0]):
        total += jnp.where(chosen[slot] == offset, products[slot], 0.0)
    return total


def spread_kernel(size, offsets, place, own_table, other_table, products, *terms):
    chosen = distances(place, own_table, other_table, size)
    for term, offset in zip(terms, offsets, strict=True):
        term[...] = gathered(chosen, products, offset).astype(term.dtype)


def update_kernel(mask, hidden, down, feats, updated):
    experts, inner, width = down.shape
    total = feats[...].astype(F32)
    for expert in range(experts):
        masked = jnp.concatenate(
            [
                hidden[:, start : start + width] * mask[expert]
                for start in range(0, inner, width)
            ],
            axis=1,
        )
        total += jnp.dot(masked, down[expert], preferred_element_type=F32)
    updated[...] = total.astype(BF16)


def finish_kernel(
    place,
    own,
    up,
    down,
    weight,
    out_grad,
    own_part,
    own_swapped,
    other_part,
    other_swapped,
    result,
    weight_grad,
):
    grad_msg = (own[...] + up[...].astype(F32) + down[...].astype(F32)).astype(BF16)
    back = lax.dot_general(grad_msg, weight[...], NT, preferred_element_type=F32)
    result[...] = (out_grad[...].astype(F32) + back).astype(BF16)
    half = own_part.shape[0]
    upper = own_part[...].astype(F32) + own_swapped[...].astype(F32)
    lower = other_part[...].astype(F32) + other_swapped[...].astype(F32)
    weight_grad[:half] = jnp.where(place[0] == 0, upper, lower)
    weight_grad[half:] = jnp.where(place[0] == 0, lower, upper)


def per_device(
    feats, msg_weight, tiles, tile_step, tile_count, node_type, expert_up, expert_down, out_grad
):
    size = lax.axis_size("grid")
    core = lax.axis_index("rep")
    chip = lax.axis_index("grid")
    order = ring_order(size)
    far = size // 2
    slots = tiles.shape[2]
    block, width = feats.shape
    half = block // 2
    cut = half // 2
    experts, _, inner = expert_up.shape

    own_feats = lax.dynamic_slice_in_dim(feats, core * half, half, 0)

    place = jnp.stack([core, chip]).astype(jnp.int32)
    tile_own, _ = lax.optimization_barrier((tiles[0, 0], own_feats))
    own_table = jnp.stack([tile_step[0, 0], tile_count[0, 0]])
    other_table = other_core(own_table)
    tile_other = other_core(tile_own)
    flip = functools.partial(call, flip_kernel, struct(tile_own.shape, BF16), ())

    mask, grad_hidden = call(
        prepare_kernel,
        [struct((experts, half, width), BF16), struct((half, inner), F32)],
        (place,),
        (node_type, out_grad, expert_down),
        (pltpu.VMEM((block, 8), F32),),
        flops=2 * experts * half * width * inner,
    )
    arrived = [(0, 0, own_feats)]
    up = down = own_feats
    for step in range(1, far):
        if step == 2:
            up, down, other_table = lax.optimization_barrier((up, down, other_table))
        if step == 3:
            up, down, mask, grad_hidden = lax.optimization_barrier((up, down, mask, grad_hidden))
        up, down = along_ring(up, order, 1), along_ring(down, order, -1)
        arrived += [(size - step, 0, up), (step, 0, down)]
    tables = (place, own_table, other_table)
    arrived += [(far, 0, along_ring(up[:cut], order, 1))]
    arrived += [(far, cut, along_ring(down[cut:], order, -1))]
    source_rows = call(
        functools.partial(pick_kernel, size, [item[:2] for item in arrived]),
        struct((2 * slots, half, width), BF16),
        tables,
        [piece for _, _, piece in arrived],
    )
    other_rows = other_core(source_rows)
    late_own, late_other, _ = lax.optimization_barrier((tile_own, tile_other, source_rows))
    flipped_own, flipped_other = flip((late_own,)), flip((late_other,))

    hidden, packed, kept = call(
        middle_kernel,
        [
            struct((half, inner), BF16),
            struct((half + width, width), BF16),
            struct((width // 2, width), F32),
        ],
        tables,
        (
            tile_own,
            tile_other,
            source_rows,
            other_rows,
            msg_weight,
            mask,
            expert_up,
            grad_hidden,
        ),
        (
            pltpu.VMEM((2 * slots, block, width), BF16),
            pltpu.VMEM((half, experts * width), BF16),
        ),
        flops=4 * half * width * (slots * block + experts * inner),
    )
    other_packed = other_core(packed)

    whole = struct((half, width), BF16)
    near = [far - 1, size - far + 1]
    products, up, down, mine, *terms = call(
        functools.partial(product_kernel, size, near),
        [
            struct((2 * slots, half, width), F32),
            struct((cut, width), BF16),
            struct((half - cut, width), BF16),
            struct((width // 2, width), BF16),
            whole,
            whole,
        ],
        tables,
        (flipped_own, flipped_other, packed, other_packed, kept),
        (pltpu.VMEM((block, width), BF16),),
        flops=4 * half * width * slots * block,
    )
    up, down = along_ring(up, order, 1), along_ring(down, order, -1)
    products = lax.optimization_barrier((products, up, down))[0]
    keys = [0]
    for step in range(far - 2, 0, -1):
        keys += [step, size - step]
    terms += call(
        functools.partial(spread_kernel, size, keys),
        [struct((half, width), F32 if key == 0 else BF16) for key in keys],
        tables,
        (products,),
    )
    terms = dict(zip(near + keys, terms, strict=True))

    def joined(received, term):
        return (received.astype(F32) + term.astype(F32)).astype(BF16)

    swap = size // 2
    while swap > 4:
        mine = joined(mine, swapped(mine, swap))
        swap //= 2
    four = (swapped(mine, swap), swapped(mine, swap // 2), swapped(mine, swap + swap // 2))
    up, down = jnp.pad(up, ((0, half - cut), (0, 0))), jnp.pad(down, ((cut, 0), (0, 0)))
    for step in range(far - 1, 0, -1):
        up, down = joined(up, terms[step]), joined(down, terms[size - step])
        if step == 1:
            *four, _, _ = lax.optimization_barrier((*four, up, down))
            four = [item.astype(F32) for item in (mine, *four)]
            mine = ((four[0] + four[1]) + (four[2] + four[3])).astype(BF16)
            weight_parts = (mine, swapped(mine, 1), other_core(mine), swapped(mine, 1, across=True))
        up, down = along_ring(up, order, 1), along_ring(down, order, -1)
        if step == far - 1:
            hidden = lax.optimization_barrier((hidden, up))[0]

    updated = call(
        update_kernel,
        struct((half, width), BF16),
        (),
        (mask, hidden, expert_down, own_feats),
        flops=2 * experts * half * width * inner,
    )
    feats_grad, msg_weight_grad = call(
        finish_kernel,
        [struct((half, width), BF16), struct((width, width), F32)],
        (place,),
        (
            terms[0],
            up,
            down,
            msg_weight,
            out_grad,
            *weight_parts,
        ),
    )
    return (updated, feats_grad, msg_weight_grad)


def solution(mesh):
    return jax.shard_map(
        per_device,
        mesh=mesh,
        in_specs=(
            P(("groups", "grid"), None),
            P(),
            P(("groups", "grid"), "rep", None, None, None),
            P(("groups", "grid"), "rep", None),
            P(("groups", "grid"), "rep", None),
            P(("groups", "grid")),
            P(),
            P(),
            P(("groups", "grid", "rep"), None),
        ),
        out_specs=(
            P(("groups", "grid", "rep"), None),
            P(("groups", "grid", "rep"), None),
            P("groups", None),
        ),
        check_vma=False,
    )
```

```python
import functools
import math

import jax
import jax.numpy as jnp
from jax import lax
from jax.experimental import pallas as pl
from jax.experimental.pallas import tpu as pltpu
from jax.sharding import PartitionSpec as P

BF16 = jnp.bfloat16
F32 = jnp.float32
NT = (((1,), (1,)), ((), ()))
TN = (((0,), (0,)), ((), ()))
SPARE_VMEM = 8 * 1024 * 1024


def ring_order(size):
    if size <= 8:
        return list(range(0, size, 2)) + list(range(1, size, 2))[::-1]
    return list(range(size))


def along_ring(block, order, hop):
    size = len(order)
    route = [(order[place], order[(place + hop) % size]) for place in range(size)]
    return lax.ppermute(block, "grid", route)


def other_core(block):
    return lax.ppermute(block, "rep", [(0, 1), (1, 0)])


def swapped(block, distance):
    return lax.ppermute(block, "grid", [(i, i ^ distance) for i in range(lax.axis_size("grid"))])


def call(kernel, out_shape, smem, vmem, scratch=(), flops=0, space=pltpu.VMEM):
    held = (*vmem, *jax.tree.leaves(out_shape))
    moved = sum(math.prod(item.shape) * item.dtype.itemsize for item in held)
    spare = sum(math.prod(item.shape) * 4 for item in scratch) + SPARE_VMEM
    return pl.pallas_call(
        kernel,
        out_shape=out_shape,
        in_specs=[pl.BlockSpec(memory_space=pltpu.SMEM)] * len(smem)
        + [pl.BlockSpec(memory_space=space)] * len(vmem),
        out_specs=jax.tree.map(lambda _: pl.BlockSpec(memory_space=pltpu.VMEM), out_shape),
        scratch_shapes=list(scratch),
        compiler_params=pltpu.CompilerParams(vmem_limit_bytes=moved + spare),
        cost_estimate=pl.CostEstimate(flops=flops, bytes_accessed=moved, transcendentals=0),
    )(*smem, *vmem)


def struct(shape, dtype):
    return jax.ShapeDtypeStruct(shape, dtype)


def ring_place(chip, size):
    if size <= 8:
        return jnp.where(lax.rem(chip, 2) == 0, lax.div(chip, 2), size - 1 - lax.div(chip, 2))
    return chip


def distances(place, own_table, other_table, size):
    core, chip = place[0], place[1]
    slots = own_table.shape[1]
    found = []
    for replica in range(2):
        for slot in range(slots):
            step = jnp.where(core == replica, own_table[0, slot], other_table[0, slot])
            source = lax.rem(chip - replica * (size // 2) - step + 2 * size, size)
            found.append(lax.rem(ring_place(source, size) - ring_place(chip, size) + size, size))
    return found


def edge_counts(place, own_table, other_table):
    core = place[0]
    slots = own_table.shape[1]
    return [
        jnp.where(core == replica, own_table[1, slot], other_table[1, slot]).astype(F32)
        for replica in range(2)
        for slot in range(slots)
    ]


def split_kernel(place, tile, sent_rows, own_flipped, sent_flipped, flipped):
    half = sent_rows.shape[1]
    own = pl.ds(pl.multiple_of(place[0] * half, half), half)
    other = pl.ds(pl.multiple_of((1 - place[0]) * half, half), half)
    for slot in range(tile.shape[0]):
        sent_rows[slot] = tile[slot, other, :]
        flipped[...] = jnp.swapaxes(tile[slot], 0, 1)
        own_flipped[slot] = flipped[own, :]
        sent_flipped[slot] = flipped[other, :]


def pick_kernel(size, offsets, place, own_table, other_table, *refs):
    blocks, rows = refs[:-1], refs[-1]
    chosen = distances(place, own_table, other_table, size)
    for slot in range(rows.shape[0]):
        for block, (offset, start) in zip(blocks, offsets, strict=True):

            @pl.when(chosen[slot] == offset)
            def _(slot=slot, block=block, start=start):
                rows[slot, pl.ds(start, block.shape[0]), :] = block[...]


def prepare_kernel(place, types, out_grad, down, mask, grad_hidden, column):
    experts, half, width = mask.shape
    block = types.shape[0]
    row = types[...].astype(F32).reshape(1, block)
    column[...] = jnp.swapaxes(jnp.broadcast_to(row, (8, block)), 0, 1)
    own = column[pl.ds(pl.multiple_of(place[0] * half, half), half), 0:1]
    own = jnp.broadcast_to(own, (half, width))
    total = None
    for expert in range(experts):
        mask[expert] = jnp.where(own == expert, 1.0, 0.0).astype(BF16)
        term = lax.dot_general(
            out_grad[...] * mask[expert], down[expert], NT, preferred_element_type=F32
        )
        total = term if total is None else total + term
    grad_hidden[...] = total


def middle_kernel(
    place,
    own_table,
    other_table,
    own_tile,
    other_tile,
    own_rows,
    other_rows,
    weight,
    mask,
    up,
    grad_hidden,
    hidden,
    packed,
    kept,
    rows,
    wide,
):
    slots = own_tile.shape[0]
    experts, width, inner = up.shape
    half = own_rows.shape[1]
    core = place[0]
    own_start = pl.multiple_of(core * half, half)
    other_start = pl.multiple_of((1 - core) * half, half)
    for slot in range(2 * slots):
        rows[slot, pl.ds(own_start, half), :] = own_rows[slot]
        rows[slot, pl.ds(other_start, half), :] = other_rows[slot]
    total = jnp.zeros((half, width), F32)
    for slot in range(slots):
        for tile_rows, table, which in (
            (own_tile[slot, pl.ds(own_start, half), :], own_table, core),
            (other_tile[slot], other_table, 1 - core),
        ):
            total += table[1, slot].astype(F32) * jnp.dot(
                tile_rows,
                rows[which * slots + slot],
                preferred_element_type=F32,
            )
    high = total.astype(BF16)
    rest = (total - high.astype(F32)).astype(BF16)
    aggregate = jnp.dot(high, weight[...], preferred_element_type=F32)
    aggregate += jnp.dot(rest, weight[...], preferred_element_type=F32)
    edges = jnp.full((1, 1), sum(edge_counts(place, own_table, other_table)), F32)
    aggregate = aggregate / edges
    inv_rms = lax.rsqrt(jnp.mean(aggregate * aggregate, axis=-1, keepdims=True) + 1e-06)
    normed = aggregate * inv_rms
    normed_bf = normed.astype(BF16)
    for expert in range(experts):
        wide[:, expert * width : (expert + 1) * width] = normed_bf * mask[expert]
    up_act = jnp.dot(
        wide[...], up[...].reshape(experts * width, inner), preferred_element_type=F32
    )
    gate = 1.0 / (1.0 + jnp.exp(-up_act))
    hidden[...] = (up_act * gate).astype(BF16)
    grad_act = (grad_hidden[...] * gate * (1.0 + up_act * (1.0 - gate))).astype(BF16)
    grad_pre = jnp.zeros((half, width), F32)
    for expert in range(experts):
        term = lax.dot_general(grad_act, up[expert], NT, preferred_element_type=F32)
        grad_pre += term * mask[expert].astype(F32)
    grad_agg = inv_rms * (
        grad_pre - normed * jnp.mean(grad_pre * normed, axis=-1, keepdims=True)
    )
    grad_scaled = (grad_agg / edges).astype(BF16)
    packed[:half] = grad_scaled
    term = lax.dot_general(high, grad_scaled, TN, preferred_element_type=F32)
    upper, lower = term[: width // 2], term[width // 2 :]
    kept[...] = jnp.where(core == 0, upper, lower)
    sent = jnp.where(core == 0, lower, upper)
    packed[half : half + width // 2] = sent.astype(BF16)
    packed[half + width // 2 :] = (sent - sent.astype(BF16).astype(F32)).astype(BF16)


def product_kernel(
    size,
    offsets,
    place,
    own_table,
    other_table,
    own_flipped,
    other_flipped,
    own_packed,
    other_packed,
    kept,
    products,
    far_first,
    far_second,
    weight_part,
    *rest,
):
    terms, full_grad = rest[:-1], rest[-1]
    slots, half, _ = own_flipped.shape
    core = place[0]
    full_grad[pl.ds(pl.multiple_of(core * half, half), half), :] = own_packed[:half]
    full_grad[pl.ds(pl.multiple_of((1 - core) * half, half), half), :] = other_packed[:half]
    middle = half + kept.shape[0]
    weight_part[...] = (
        kept[...] + other_packed[half:middle].astype(F32) + other_packed[middle:].astype(F32)
    ).astype(BF16)
    for flipped, table, which in (
        (own_flipped, own_table, core),
        (other_flipped, other_table, 1 - core),
    ):
        for slot in range(slots):
            products[which * slots + slot] = table[1, slot].astype(F32) * jnp.dot(
                flipped[slot], full_grad[...], preferred_element_type=F32
            )
    chosen = distances(place, own_table, other_table, size)
    total = gathered(chosen, products, size // 2)
    cut = far_first.shape[0]
    far_first[...] = total[:cut].astype(BF16)
    far_second[...] = total[cut:].astype(BF16)
    for term, offset in zip(terms, offsets, strict=True):
        term[...] = gathered(chosen, products, offset).astype(BF16)


def gathered(chosen, products, offset):
    total = jnp.where(chosen[0] == offset, products[0], 0.0)
    for slot in range(1, products.shape[0]):
        total += jnp.where(chosen[slot] == offset, products[slot], 0.0)
    return total


def spread_kernel(size, offsets, place, own_table, other_table, products, *terms):
    chosen = distances(place, own_table, other_table, size)
    for term, offset in zip(terms, offsets, strict=True):
        term[...] = gathered(chosen, products, offset).astype(term.dtype)


def update_kernel(mask, hidden, down, feats, updated):
    experts, inner, width = down.shape
    total = feats[...].astype(F32)
    for expert in range(experts):
        masked = jnp.concatenate(
            [
                hidden[:, start : start + width] * mask[expert]
                for start in range(0, inner, width)
            ],
            axis=1,
        )
        total += jnp.dot(masked, down[expert], preferred_element_type=F32)
    updated[...] = total.astype(BF16)


def finish_kernel(
    place,
    own,
    up,
    down,
    weight,
    out_grad,
    own_total,
    other_total,
    result,
    weight_grad,
):
    grad_msg = (own[...] + up[...].astype(F32) + down[...].astype(F32)).astype(BF16)
    back = lax.dot_general(grad_msg, weight[...], NT, preferred_element_type=F32)
    result[...] = (out_grad[...].astype(F32) + back).astype(BF16)
    half = own_total.shape[0]
    upper, lower = own_total[...], other_total[...]
    weight_grad[:half] = jnp.where(place[0] == 0, upper, lower)
    weight_grad[half:] = jnp.where(place[0] == 0, lower, upper)


def per_device(
    feats, msg_weight, tiles, tile_step, tile_count, node_type, expert_up, expert_down, out_grad
):
    size = lax.axis_size("grid")
    core = lax.axis_index("rep")
    chip = lax.axis_index("grid")
    order = ring_order(size)
    far = size // 2
    slots = tiles.shape[2]
    block, width = feats.shape
    half = block // 2
    cut = half // 2
    experts, _, inner = expert_up.shape

    own_feats = lax.dynamic_slice_in_dim(feats, core * half, half, 0)

    place = jnp.stack([core, chip]).astype(jnp.int32)
    tile_own = tiles[0, 0]
    own_table = jnp.stack([tile_step[0, 0], tile_count[0, 0]])
    other_table = other_core(own_table)

    mask, grad_hidden = call(
        prepare_kernel,
        [struct((experts, half, width), BF16), struct((half, inner), F32)],
        (place,),
        (node_type, out_grad, expert_down),
        (pltpu.VMEM((block, 8), F32),),
        flops=2 * experts * half * width * inner,
    )
    arrived = [(0, 0, own_feats)]
    up = down = own_feats
    for step in range(1, far):
        if step == 2:
            up, down, other_table = lax.optimization_barrier((up, down, other_table))
        if step == 3:
            up, down, mask, grad_hidden = lax.optimization_barrier((up, down, mask, grad_hidden))
        if step == min(3, far - 1):
            tile_late = lax.optimization_barrier((tile_own, up, down))[0]
            sent_rows, flipped_own, sent_flipped = call(
                split_kernel,
                [struct((slots, half, block), BF16)] * 3,
                (place,),
                (tile_late,),
                (pltpu.VMEM((block, block), BF16),),
            )
            tile_other = other_core(sent_rows)
        if step % 2:
            up, down = along_ring(up, order, 1), along_ring(down, order, -1)
        else:
            down, up = along_ring(down, order, -1), along_ring(up, order, 1)
        arrived += [(size - step, 0, up), (step, 0, down)]
    tables = (place, own_table, other_table)
    arrived += [(far, cut, along_ring(down[cut:], order, -1))]
    arrived += [(far, 0, along_ring(up[:cut], order, 1))]
    source_rows = call(
        functools.partial(pick_kernel, size, [item[:2] for item in arrived]),
        struct((2 * slots, half, width), BF16),
        tables,
        [piece for _, _, piece in arrived],
    )
    other_rows = other_core(source_rows)
    flipped_other = other_core(lax.optimization_barrier((sent_flipped, other_rows))[0])

    hidden, packed, kept = call(
        middle_kernel,
        [
            struct((half, inner), BF16),
            struct((half + width, width), BF16),
            struct((width // 2, width), F32),
        ],
        tables,
        (
            tile_own,
            tile_other,
            source_rows,
            other_rows,
            msg_weight,
            mask,
            expert_up,
            grad_hidden,
        ),
        (
            pltpu.VMEM((2 * slots, block, width), BF16),
            pltpu.VMEM((half, experts * width), BF16),
        ),
        flops=4 * half * width * (slots * block + experts * inner),
    )
    other_packed = other_core(packed)

    whole = struct((half, width), BF16)
    near = [far - 1, size - far + 1]
    products, up, down, mine, *terms = call(
        functools.partial(product_kernel, size, near),
        [
            struct((2 * slots, half, width), F32),
            struct((cut, width), BF16),
            struct((half - cut, width), BF16),
            struct((width // 2, width), BF16),
            whole,
            whole,
        ],
        tables,
        (flipped_own, flipped_other, packed, other_packed, kept),
        (pltpu.VMEM((block, width), BF16),),
        flops=4 * half * width * slots * block,
    )
    up, down = along_ring(up, order, 1), along_ring(down, order, -1)
    products = lax.optimization_barrier((products, up, down))[0]
    keys = [0]
    for step in range(far - 2, 0, -1):
        keys += [step, size - step]
    terms += call(
        functools.partial(spread_kernel, size, keys),
        [struct((half, width), F32 if key == 0 else BF16) for key in keys],
        tables,
        (products,),
    )
    terms = dict(zip(near + keys, terms, strict=True))

    def added(mine, theirs):
        values = [mine.astype(F32)] + [item.astype(F32) for item in theirs]
        while len(values) > 1:
            values = [values[i] + values[i + 1] for i in range(0, len(values), 2)]
        return values[0]

    def joined(received, term):
        return (received.astype(F32) + term.astype(F32)).astype(BF16)

    swaps = [(1, 2, 3)] + [(1 << bit,) for bit in range(2, size.bit_length() - 1)]
    theirs = [swapped(mine, distance) for distance in swaps.pop(0)]
    total = None
    up, down = jnp.pad(up, ((0, half - cut), (0, 0))), jnp.pad(down, ((cut, 0), (0, 0)))
    for step in range(far - 1, 0, -1):
        up, down = joined(up, terms[step]), joined(down, terms[size - step])
        if step < far - 1 and total is None:
            *theirs, _, _ = lax.optimization_barrier((*theirs, up, down))
            total = added(mine, theirs)
            if swaps:
                mine, total = total.astype(BF16), None
                theirs = [swapped(mine, distance) for distance in swaps.pop(0)]
            else:
                other_total = other_core(total)
        if step % 2:
            down, up = along_ring(down, order, -1), along_ring(up, order, 1)
        else:
            up, down = along_ring(up, order, 1), along_ring(down, order, -1)
        if step == far - 1:
            hidden = lax.optimization_barrier((hidden, up))[0]

    updated = call(
        update_kernel,
        struct((half, width), BF16),
        (),
        (mask, hidden, expert_down, own_feats),
        flops=2 * experts * half * width * inner,
    )
    feats_grad, msg_weight_grad = call(
        finish_kernel,
        [struct((half, width), BF16), struct((width, width), F32)],
        (place,),
        (
            terms[0],
            up,
            down,
            msg_weight,
            out_grad,
            total,
            other_total,
        ),
    )
    return (updated, feats_grad, msg_weight_grad)


def solution(mesh):
    return jax.shard_map(
        per_device,
        mesh=mesh,
        in_specs=(
            P(("groups", "grid"), None),
            P(),
            P(("groups", "grid"), "rep", None, None, None),
            P(("groups", "grid"), "rep", None),
            P(("groups", "grid"), "rep", None),
            P(("groups", "grid")),
            P(),
            P(),
            P(("groups", "grid", "rep"), None),
        ),
        out_specs=(
            P(("groups", "grid", "rep"), None),
            P(("groups", "grid", "rep"), None),
            P("groups", None),
        ),
        check_vma=False,
    )
```

```python
import functools
import math

import jax
import jax.numpy as jnp
from jax import lax
from jax.experimental import pallas as pl
from jax.experimental.pallas import tpu as pltpu
from jax.sharding import PartitionSpec as P

BF16 = jnp.bfloat16
F32 = jnp.float32
NT = (((1,), (1,)), ((), ()))
TN = (((0,), (0,)), ((), ()))
SPARE_VMEM = 8 * 1024 * 1024


def ring_order(size):
    if size <= 8:
        return list(range(0, size, 2)) + list(range(1, size, 2))[::-1]
    return list(range(size))


def along_ring(block, order, hop):
    size = len(order)
    route = [(order[place], order[(place + hop) % size]) for place in range(size)]
    return lax.ppermute(block, "grid", route)


def other_core(block):
    return lax.ppermute(block, "rep", [(0, 1), (1, 0)])


def swapped(block, distance):
    return lax.ppermute(block, "grid", [(i, i ^ distance) for i in range(lax.axis_size("grid"))])


def call(kernel, out_shape, smem, vmem, scratch=(), flops=0, space=pltpu.VMEM):
    held = (*vmem, *jax.tree.leaves(out_shape))
    moved = sum(math.prod(item.shape) * item.dtype.itemsize for item in held)
    spare = sum(math.prod(item.shape) * 4 for item in scratch) + SPARE_VMEM
    return pl.pallas_call(
        kernel,
        out_shape=out_shape,
        in_specs=[pl.BlockSpec(memory_space=pltpu.SMEM)] * len(smem)
        + [pl.BlockSpec(memory_space=space)] * len(vmem),
        out_specs=jax.tree.map(lambda _: pl.BlockSpec(memory_space=pltpu.VMEM), out_shape),
        scratch_shapes=list(scratch),
        compiler_params=pltpu.CompilerParams(vmem_limit_bytes=moved + spare),
        cost_estimate=pl.CostEstimate(flops=flops, bytes_accessed=moved, transcendentals=0),
    )(*smem, *vmem)


def struct(shape, dtype):
    return jax.ShapeDtypeStruct(shape, dtype)


def ring_place(chip, size):
    if size <= 8:
        return jnp.where(lax.rem(chip, 2) == 0, lax.div(chip, 2), size - 1 - lax.div(chip, 2))
    return chip


def distances(place, own_table, other_table, size):
    core, chip = place[0], place[1]
    slots = own_table.shape[1]
    found = []
    for replica in range(2):
        for slot in range(slots):
            step = jnp.where(core == replica, own_table[0, slot], other_table[0, slot])
            source = lax.rem(chip - replica * (size // 2) - step + 2 * size, size)
            found.append(lax.rem(ring_place(source, size) - ring_place(chip, size) + size, size))
    return found


def edge_counts(place, own_table, other_table):
    core = place[0]
    slots = own_table.shape[1]
    return [
        jnp.where(core == replica, own_table[1, slot], other_table[1, slot]).astype(F32)
        for replica in range(2)
        for slot in range(slots)
    ]


def split_kernel(place, tile, sent_rows, own_flipped, sent_flipped, flipped):
    half = sent_rows.shape[1]
    own = pl.ds(pl.multiple_of(place[0] * half, half), half)
    other = pl.ds(pl.multiple_of((1 - place[0]) * half, half), half)
    for slot in range(tile.shape[0]):
        sent_rows[slot] = tile[slot, other, :]
        flipped[...] = jnp.swapaxes(tile[slot], 0, 1)
        own_flipped[slot] = flipped[own, :]
        sent_flipped[slot] = flipped[other, :]


def pick_kernel(size, offsets, place, own_table, other_table, *refs):
    blocks, rows = refs[:-1], refs[-1]
    chosen = distances(place, own_table, other_table, size)
    for slot in range(rows.shape[0]):
        for block, (offset, start) in zip(blocks, offsets, strict=True):

            @pl.when(chosen[slot] == offset)
            def _(slot=slot, block=block, start=start):
                rows[slot, pl.ds(start, block.shape[0]), :] = block[...]


def prepare_kernel(place, types, out_grad, down, mask, grad_hidden, column):
    experts, half, width = mask.shape
    block = types.shape[0]
    row = types[...].astype(F32).reshape(1, block)
    column[...] = jnp.swapaxes(jnp.broadcast_to(row, (8, block)), 0, 1)
    own = column[pl.ds(pl.multiple_of(place[0] * half, half), half), 0:1]
    own = jnp.broadcast_to(own, (half, width))
    total = None
    for expert in range(experts):
        mask[expert] = jnp.where(own == expert, 1.0, 0.0).astype(BF16)
        term = lax.dot_general(
            out_grad[...] * mask[expert], down[expert], NT, preferred_element_type=F32
        )
        total = term if total is None else total + term
    grad_hidden[...] = total


def middle_kernel(
    place,
    own_table,
    other_table,
    own_tile,
    other_tile,
    own_rows,
    other_rows,
    weight,
    mask,
    up,
    grad_hidden,
    hidden,
    packed,
    kept,
    rows,
    wide,
):
    slots = own_tile.shape[0]
    experts, width, inner = up.shape
    half = own_rows.shape[1]
    core = place[0]
    own_start = pl.multiple_of(core * half, half)
    other_start = pl.multiple_of((1 - core) * half, half)
    for slot in range(2 * slots):
        rows[slot, pl.ds(own_start, half), :] = own_rows[slot]
        rows[slot, pl.ds(other_start, half), :] = other_rows[slot]
    total = jnp.zeros((half, width), F32)
    for slot in range(slots):
        for tile_rows, table, which in (
            (own_tile[slot, pl.ds(own_start, half), :], own_table, core),
            (other_tile[slot], other_table, 1 - core),
        ):
            total += table[1, slot].astype(F32) * jnp.dot(
                tile_rows,
                rows[which * slots + slot],
                preferred_element_type=F32,
            )
    high = total.astype(BF16)
    rest = (total - high.astype(F32)).astype(BF16)
    aggregate = jnp.dot(high, weight[...], preferred_element_type=F32)
    aggregate += jnp.dot(rest, weight[...], preferred_element_type=F32)
    edges = jnp.full((1, 1), sum(edge_counts(place, own_table, other_table)), F32)
    aggregate = aggregate / edges
    inv_rms = lax.rsqrt(jnp.mean(aggregate * aggregate, axis=-1, keepdims=True) + 1e-06)
    normed = aggregate * inv_rms
    normed_bf = normed.astype(BF16)
    for expert in range(experts):
        wide[:, expert * width : (expert + 1) * width] = normed_bf * mask[expert]
    up_act = jnp.dot(
        wide[...], up[...].reshape(experts * width, inner), preferred_element_type=F32
    )
    gate = 1.0 / (1.0 + jnp.exp(-up_act))
    hidden[...] = (up_act * gate).astype(BF16)
    grad_act = (grad_hidden[...] * gate * (1.0 + up_act * (1.0 - gate))).astype(BF16)
    grad_pre = jnp.zeros((half, width), F32)
    for expert in range(experts):
        term = lax.dot_general(grad_act, up[expert], NT, preferred_element_type=F32)
        grad_pre += term * mask[expert].astype(F32)
    grad_agg = inv_rms * (
        grad_pre - normed * jnp.mean(grad_pre * normed, axis=-1, keepdims=True)
    )
    grad_scaled = (grad_agg / edges).astype(BF16)
    packed[:half] = grad_scaled
    term = lax.dot_general(high, grad_scaled, TN, preferred_element_type=F32)
    upper, lower = term[: width // 2], term[width // 2 :]
    kept[...] = jnp.where(core == 0, upper, lower)
    sent = jnp.where(core == 0, lower, upper)
    packed[half : half + width // 2] = sent.astype(BF16)
    packed[half + width // 2 :] = (sent - sent.astype(BF16).astype(F32)).astype(BF16)


def product_kernel(
    size,
    offsets,
    place,
    own_table,
    other_table,
    own_flipped,
    other_flipped,
    own_packed,
    other_packed,
    kept,
    products,
    far_first,
    far_second,
    weight_part,
    *rest,
):
    terms, full_grad = rest[:-1], rest[-1]
    slots, half, _ = own_flipped.shape
    core = place[0]
    full_grad[pl.ds(pl.multiple_of(core * half, half), half), :] = own_packed[:half]
    full_grad[pl.ds(pl.multiple_of((1 - core) * half, half), half), :] = other_packed[:half]
    middle = half + kept.shape[0]
    weight_part[...] = (
        kept[...] + other_packed[half:middle].astype(F32) + other_packed[middle:].astype(F32)
    ).astype(BF16)
    for flipped, table, which in (
        (own_flipped, own_table, core),
        (other_flipped, other_table, 1 - core),
    ):
        for slot in range(slots):
            products[which * slots + slot] = table[1, slot].astype(F32) * jnp.dot(
                flipped[slot], full_grad[...], preferred_element_type=F32
            )
    chosen = distances(place, own_table, other_table, size)
    total = gathered(chosen, products, size // 2)
    cut = far_first.shape[0]
    far_first[...] = total[:cut].astype(BF16)
    far_second[...] = total[cut:].astype(BF16)
    for term, offset in zip(terms, offsets, strict=True):
        term[...] = gathered(chosen, products, offset).astype(BF16)


def gathered(chosen, products, offset):
    total = jnp.where(chosen[0] == offset, products[0], 0.0)
    for slot in range(1, products.shape[0]):
        total += jnp.where(chosen[slot] == offset, products[slot], 0.0)
    return total


def spread_kernel(size, offsets, place, own_table, other_table, products, *terms):
    chosen = distances(place, own_table, other_table, size)
    for term, offset in zip(terms, offsets, strict=True):
        term[...] = gathered(chosen, products, offset).astype(term.dtype)


def update_kernel(mask, hidden, down, feats, updated):
    experts, inner, width = down.shape
    total = feats[...].astype(F32)
    for expert in range(experts):
        masked = jnp.concatenate(
            [
                hidden[:, start : start + width] * mask[expert]
                for start in range(0, inner, width)
            ],
            axis=1,
        )
        total += jnp.dot(masked, down[expert], preferred_element_type=F32)
    updated[...] = total.astype(BF16)


def finish_kernel(own, up, down, weight, out_grad, result):
    grad_msg = (own[...] + up[...].astype(F32) + down[...].astype(F32)).astype(BF16)
    back = lax.dot_general(grad_msg, weight[...], NT, preferred_element_type=F32)
    result[...] = (out_grad[...].astype(F32) + back).astype(BF16)


def weight_kernel(place, own_total, other_total, weight_grad):
    half = own_total.shape[0]
    upper, lower = own_total[...], other_total[...]
    weight_grad[:half] = jnp.where(place[0] == 0, upper, lower)
    weight_grad[half:] = jnp.where(place[0] == 0, lower, upper)


def per_device(
    feats, msg_weight, tiles, tile_step, tile_count, node_type, expert_up, expert_down, out_grad
):
    size = lax.axis_size("grid")
    core = lax.axis_index("rep")
    chip = lax.axis_index("grid")
    order = ring_order(size)
    far = size // 2
    slots = tiles.shape[2]
    block, width = feats.shape
    half = block // 2
    cut = half // 2
    experts, _, inner = expert_up.shape

    own_feats = lax.dynamic_slice_in_dim(feats, core * half, half, 0)

    place = jnp.stack([core, chip]).astype(jnp.int32)
    tile_own = tiles[0, 0]
    own_table = jnp.stack([tile_step[0, 0], tile_count[0, 0]])
    other_table = other_core(own_table)

    mask, grad_hidden = call(
        prepare_kernel,
        [struct((experts, half, width), BF16), struct((half, inner), F32)],
        (place,),
        (node_type, out_grad, expert_down),
        (pltpu.VMEM((block, 8), F32),),
        flops=2 * experts * half * width * inner,
    )
    arrived = [(0, 0, own_feats)]
    up = down = own_feats
    for step in range(1, far):
        if step == 2:
            up, down, other_table = lax.optimization_barrier((up, down, other_table))
        if step == 3:
            up, down, mask, grad_hidden = lax.optimization_barrier((up, down, mask, grad_hidden))
        if step == min(3, far - 1):
            tile_late = lax.optimization_barrier((tile_own, up, down))[0]
            sent_rows, flipped_own, sent_flipped = call(
                split_kernel,
                [struct((slots, half, block), BF16)] * 3,
                (place,),
                (tile_late,),
                (pltpu.VMEM((block, block), BF16),),
            )
            tile_other = other_core(sent_rows)
        if step % 2:
            up, down = along_ring(up, order, 1), along_ring(down, order, -1)
        else:
            down, up = along_ring(down, order, -1), along_ring(up, order, 1)
        arrived += [(size - step, 0, up), (step, 0, down)]
    tables = (place, own_table, other_table)
    arrived += [(far, cut, along_ring(down[cut:], order, -1))]
    arrived += [(far, 0, along_ring(up[:cut], order, 1))]
    source_rows = call(
        functools.partial(pick_kernel, size, [item[:2] for item in arrived]),
        struct((2 * slots, half, width), BF16),
        tables,
        [piece for _, _, piece in arrived],
    )
    other_rows = other_core(source_rows)
    flipped_other = other_core(lax.optimization_barrier((sent_flipped, other_rows))[0])

    hidden, packed, kept = call(
        middle_kernel,
        [
            struct((half, inner), BF16),
            struct((half + width, width), BF16),
            struct((width // 2, width), F32),
        ],
        tables,
        (
            tile_own,
            tile_other,
            source_rows,
            other_rows,
            msg_weight,
            mask,
            expert_up,
            grad_hidden,
        ),
        (
            pltpu.VMEM((2 * slots, block, width), BF16),
            pltpu.VMEM((half, experts * width), BF16),
        ),
        flops=4 * half * width * (slots * block + experts * inner),
    )
    other_packed = other_core(packed)

    whole = struct((half, width), BF16)
    near = [far - 1, size - far + 1]
    products, up, down, mine, *terms = call(
        functools.partial(product_kernel, size, near),
        [
            struct((2 * slots, half, width), F32),
            struct((cut, width), BF16),
            struct((half - cut, width), BF16),
            struct((width // 2, width), BF16),
            whole,
            whole,
        ],
        tables,
        (flipped_own, flipped_other, packed, other_packed, kept),
        (pltpu.VMEM((block, width), BF16),),
        flops=4 * half * width * slots * block,
    )
    up, down = along_ring(up, order, 1), along_ring(down, order, -1)
    products = lax.optimization_barrier((products, up, down))[0]
    keys = [0]
    for step in range(far - 2, 0, -1):
        keys += [step, size - step]
    terms += call(
        functools.partial(spread_kernel, size, keys),
        [struct((half, width), F32 if key == 0 else BF16) for key in keys],
        tables,
        (products,),
    )
    terms = dict(zip(near + keys, terms, strict=True))

    def added(mine, theirs):
        values = [mine.astype(F32)] + [item.astype(F32) for item in theirs]
        while len(values) > 1:
            values = [values[i] + values[i + 1] for i in range(0, len(values), 2)]
        return values[0]

    def joined(received, term):
        return (received.astype(F32) + term.astype(F32)).astype(BF16)

    swaps = [(1, 2, 3)] + [(1 << bit,) for bit in range(2, size.bit_length() - 1)]
    theirs = [swapped(mine, distance) for distance in swaps.pop(0)]
    total = None
    up, down = jnp.pad(up, ((0, half - cut), (0, 0))), jnp.pad(down, ((cut, 0), (0, 0)))
    for step in range(far - 1, 0, -1):
        up, down = joined(up, terms[step]), joined(down, terms[size - step])
        if step < far - 1 and total is None:
            behind = (up, down) if step < far - 2 else (terms[step], terms[size - step])
            *theirs, _, _ = lax.optimization_barrier((*theirs, *behind))
            total = added(mine, theirs)
            if swaps:
                mine, total = total.astype(BF16), None
                theirs = [swapped(mine, distance) for distance in swaps.pop(0)]
            else:
                other_total = other_core(total)
        if step % 2:
            down, up = along_ring(down, order, -1), along_ring(up, order, 1)
        else:
            up, down = along_ring(up, order, 1), along_ring(down, order, -1)
        if step == far - 1:
            hidden = lax.optimization_barrier((hidden, up))[0]

    updated = call(
        update_kernel,
        struct((half, width), BF16),
        (),
        (mask, hidden, expert_down, own_feats),
        flops=2 * experts * half * width * inner,
    )
    msg_weight_grad = call(
        weight_kernel, struct((width, width), F32), (place,), (total, other_total)
    )
    feats_grad = call(
        finish_kernel,
        struct((half, width), BF16),
        (),
        (terms[0], up, down, msg_weight, out_grad),
        flops=2 * half * width * width,
    )
    return (updated, feats_grad, msg_weight_grad)


def solution(mesh):
    return jax.shard_map(
        per_device,
        mesh=mesh,
        in_specs=(
            P(("groups", "grid"), None),
            P(),
            P(("groups", "grid"), "rep", None, None, None),
            P(("groups", "grid"), "rep", None),
            P(("groups", "grid"), "rep", None),
            P(("groups", "grid")),
            P(),
            P(),
            P(("groups", "grid", "rep"), None),
        ),
        out_specs=(
            P(("groups", "grid", "rep"), None),
            P(("groups", "grid", "rep"), None),
            P("groups", None),
        ),
        check_vma=False,
    )
```

```python
import functools
import math

import jax
import jax.numpy as jnp
from jax import lax
from jax.experimental import pallas as pl
from jax.experimental.pallas import tpu as pltpu
from jax.sharding import PartitionSpec as P

BF16 = jnp.bfloat16
F32 = jnp.float32
NT = (((1,), (1,)), ((), ()))
TN = (((0,), (0,)), ((), ()))
SPARE_VMEM = 8 * 1024 * 1024


def ring_order(size):
    if size <= 8:
        return list(range(1, size, 2)) + list(range(0, size, 2))[::-1]
    return list(range(size))


def along_ring(block, order, hop):
    size = len(order)
    route = [(order[place], order[(place + hop) % size]) for place in range(size)]
    return lax.ppermute(block, "grid", route)


def other_core(block):
    return lax.ppermute(block, "rep", [(0, 1), (1, 0)])


def swapped(block, distance):
    return lax.ppermute(block, "grid", [(i, i ^ distance) for i in range(lax.axis_size("grid"))])


def call(kernel, out_shape, smem, vmem, scratch=(), flops=0, space=pltpu.VMEM):
    held = (*vmem, *jax.tree.leaves(out_shape))
    moved = sum(math.prod(item.shape) * item.dtype.itemsize for item in held)
    spare = sum(math.prod(item.shape) * 4 for item in scratch) + SPARE_VMEM
    return pl.pallas_call(
        kernel,
        out_shape=out_shape,
        in_specs=[pl.BlockSpec(memory_space=pltpu.SMEM)] * len(smem)
        + [pl.BlockSpec(memory_space=space)] * len(vmem),
        out_specs=jax.tree.map(lambda _: pl.BlockSpec(memory_space=pltpu.VMEM), out_shape),
        scratch_shapes=list(scratch),
        compiler_params=pltpu.CompilerParams(vmem_limit_bytes=moved + spare),
        cost_estimate=pl.CostEstimate(flops=flops, bytes_accessed=moved, transcendentals=0),
    )(*smem, *vmem)


def struct(shape, dtype):
    return jax.ShapeDtypeStruct(shape, dtype)


def ring_place(chip, size):
    if size <= 8:
        return jnp.where(lax.rem(chip, 2) == 1, lax.div(chip, 2), size - 1 - lax.div(chip, 2))
    return chip


def distances(place, own_table, other_table, size):
    core, chip = place[0], place[1]
    slots = own_table.shape[1]
    found = []
    for replica in range(2):
        for slot in range(slots):
            step = jnp.where(core == replica, own_table[0, slot], other_table[0, slot])
            source = lax.rem(chip - replica * (size // 2) - step + 2 * size, size)
            found.append(lax.rem(ring_place(source, size) - ring_place(chip, size) + size, size))
    return found


def edge_counts(place, own_table, other_table):
    core = place[0]
    slots = own_table.shape[1]
    return [
        jnp.where(core == replica, own_table[1, slot], other_table[1, slot]).astype(F32)
        for replica in range(2)
        for slot in range(slots)
    ]


def split_kernel(place, tile, sent_rows, own_flipped, sent_flipped, flipped):
    half = sent_rows.shape[1]
    own = pl.ds(pl.multiple_of(place[0] * half, half), half)
    other = pl.ds(pl.multiple_of((1 - place[0]) * half, half), half)
    for slot in range(tile.shape[0]):
        sent_rows[slot] = tile[slot, other, :]
        flipped[...] = jnp.swapaxes(tile[slot], 0, 1)
        own_flipped[slot] = flipped[own, :]
        sent_flipped[slot] = flipped[other, :]


def pick_kernel(size, offsets, place, own_table, other_table, *refs):
    blocks, rows = refs[:-1], refs[-1]
    chosen = distances(place, own_table, other_table, size)
    for slot in range(rows.shape[0]):
        for block, (offset, start) in zip(blocks, offsets, strict=True):

            @pl.when(chosen[slot] == offset)
            def _(slot=slot, block=block, start=start):
                rows[slot, pl.ds(start, block.shape[0]), :] = block[...]


def prepare_kernel(place, types, out_grad, down, mask, grad_hidden, column):
    experts, half, width = mask.shape
    block = types.shape[0]
    row = types[...].astype(F32).reshape(1, block)
    column[...] = jnp.swapaxes(jnp.broadcast_to(row, (8, block)), 0, 1)
    own = column[pl.ds(pl.multiple_of(place[0] * half, half), half), 0:1]
    own = jnp.broadcast_to(own, (half, width))
    total = None
    for expert in range(experts):
        mask[expert] = jnp.where(own == expert, 1.0, 0.0).astype(BF16)
        term = lax.dot_general(
            out_grad[...] * mask[expert], down[expert], NT, preferred_element_type=F32
        )
        total = term if total is None else total + term
    grad_hidden[...] = total


def middle_kernel(
    place,
    own_table,
    other_table,
    own_tile,
    other_tile,
    own_rows,
    other_rows,
    weight,
    mask,
    up,
    grad_hidden,
    hidden,
    packed,
    kept,
    rows,
    wide,
):
    slots = own_tile.shape[0]
    experts, width, inner = up.shape
    half = own_rows.shape[1]
    core = place[0]
    own_start = pl.multiple_of(core * half, half)
    other_start = pl.multiple_of((1 - core) * half, half)
    for slot in range(2 * slots):
        rows[slot, pl.ds(own_start, half), :] = own_rows[slot]
        rows[slot, pl.ds(other_start, half), :] = other_rows[slot]
    total = jnp.zeros((half, width), F32)
    for slot in range(slots):
        for tile_rows, table, which in (
            (own_tile[slot, pl.ds(own_start, half), :], own_table, core),
            (other_tile[slot], other_table, 1 - core),
        ):
            total += table[1, slot].astype(F32) * jnp.dot(
                tile_rows,
                rows[which * slots + slot],
                preferred_element_type=F32,
            )
    high = total.astype(BF16)
    rest = (total - high.astype(F32)).astype(BF16)
    aggregate = jnp.dot(high, weight[...], preferred_element_type=F32)
    aggregate += jnp.dot(rest, weight[...], preferred_element_type=F32)
    edges = jnp.full((1, 1), sum(edge_counts(place, own_table, other_table)), F32)
    aggregate = aggregate / edges
    inv_rms = lax.rsqrt(jnp.mean(aggregate * aggregate, axis=-1, keepdims=True) + 1e-06)
    normed = aggregate * inv_rms
    normed_bf = normed.astype(BF16)
    for expert in range(experts):
        wide[:, expert * width : (expert + 1) * width] = normed_bf * mask[expert]
    up_act = jnp.dot(
        wide[...], up[...].reshape(experts * width, inner), preferred_element_type=F32
    )
    gate = 1.0 / (1.0 + jnp.exp(-up_act))
    hidden[...] = (up_act * gate).astype(BF16)
    grad_act = (grad_hidden[...] * gate * (1.0 + up_act * (1.0 - gate))).astype(BF16)
    grad_pre = jnp.zeros((half, width), F32)
    for expert in range(experts):
        term = lax.dot_general(grad_act, up[expert], NT, preferred_element_type=F32)
        grad_pre += term * mask[expert].astype(F32)
    grad_agg = inv_rms * (
        grad_pre - normed * jnp.mean(grad_pre * normed, axis=-1, keepdims=True)
    )
    grad_scaled = (grad_agg / edges).astype(BF16)
    packed[:half] = grad_scaled
    term = lax.dot_general(high, grad_scaled, TN, preferred_element_type=F32)
    upper, lower = term[: width // 2], term[width // 2 :]
    kept[...] = jnp.where(core == 0, upper, lower)
    sent = jnp.where(core == 0, lower, upper)
    packed[half : half + width // 2] = sent.astype(BF16)
    packed[half + width // 2 :] = (sent - sent.astype(BF16).astype(F32)).astype(BF16)


def product_kernel(
    size,
    offsets,
    place,
    own_table,
    other_table,
    own_flipped,
    other_flipped,
    own_packed,
    other_packed,
    kept,
    products,
    far_first,
    far_second,
    weight_part,
    *rest,
):
    terms, full_grad = rest[:-1], rest[-1]
    slots, half, _ = own_flipped.shape
    core = place[0]
    full_grad[pl.ds(pl.multiple_of(core * half, half), half), :] = own_packed[:half]
    full_grad[pl.ds(pl.multiple_of((1 - core) * half, half), half), :] = other_packed[:half]
    middle = half + kept.shape[0]
    weight_part[...] = (
        kept[...] + other_packed[half:middle].astype(F32) + other_packed[middle:].astype(F32)
    ).astype(BF16)
    for flipped, table, which in (
        (own_flipped, own_table, core),
        (other_flipped, other_table, 1 - core),
    ):
        for slot in range(slots):
            products[which * slots + slot] = table[1, slot].astype(F32) * jnp.dot(
                flipped[slot], full_grad[...], preferred_element_type=F32
            )
    chosen = distances(place, own_table, other_table, size)
    total = gathered(chosen, products, size // 2)
    cut = far_first.shape[0]
    far_first[...] = total[:cut].astype(BF16)
    far_second[...] = total[cut:].astype(BF16)
    for term, offset in zip(terms, offsets, strict=True):
        term[...] = gathered(chosen, products, offset).astype(BF16)


def gathered(chosen, products, offset):
    total = jnp.where(chosen[0] == offset, products[0], 0.0)
    for slot in range(1, products.shape[0]):
        total += jnp.where(chosen[slot] == offset, products[slot], 0.0)
    return total


def spread_kernel(size, offsets, place, own_table, other_table, products, *terms):
    chosen = distances(place, own_table, other_table, size)
    for term, offset in zip(terms, offsets, strict=True):
        term[...] = gathered(chosen, products, offset).astype(term.dtype)


def update_kernel(mask, hidden, down, feats, updated):
    experts, inner, width = down.shape
    total = feats[...].astype(F32)
    for expert in range(experts):
        masked = jnp.concatenate(
            [
                hidden[:, start : start + width] * mask[expert]
                for start in range(0, inner, width)
            ],
            axis=1,
        )
        total += jnp.dot(masked, down[expert], preferred_element_type=F32)
    updated[...] = total.astype(BF16)


def finish_kernel(own, up, down, weight, out_grad, result):
    grad_msg = (own[...] + up[...].astype(F32) + down[...].astype(F32)).astype(BF16)
    back = lax.dot_general(grad_msg, weight[...], NT, preferred_element_type=F32)
    result[...] = (out_grad[...].astype(F32) + back).astype(BF16)


def weight_kernel(place, own_total, other_total, weight_grad):
    half = own_total.shape[0]
    upper, lower = own_total[...], other_total[...]
    weight_grad[:half] = jnp.where(place[0] == 0, upper, lower)
    weight_grad[half:] = jnp.where(place[0] == 0, lower, upper)


def per_device(
    feats, msg_weight, tiles, tile_step, tile_count, node_type, expert_up, expert_down, out_grad
):
    size = lax.axis_size("grid")
    core = lax.axis_index("rep")
    chip = lax.axis_index("grid")
    order = ring_order(size)
    far = size // 2
    slots = tiles.shape[2]
    block, width = feats.shape
    half = block // 2
    cut = half // 2
    experts, _, inner = expert_up.shape

    own_feats = lax.dynamic_slice_in_dim(feats, core * half, half, 0)

    place = jnp.stack([core, chip]).astype(jnp.int32)
    tile_own = tiles[0, 0]
    own_table = jnp.stack([tile_step[0, 0], tile_count[0, 0]])
    other_table = other_core(own_table)

    mask, grad_hidden = call(
        prepare_kernel,
        [struct((experts, half, width), BF16), struct((half, inner), F32)],
        (place,),
        (node_type, out_grad, expert_down),
        (pltpu.VMEM((block, 8), F32),),
        flops=2 * experts * half * width * inner,
    )
    arrived = [(0, 0, own_feats)]
    up = down = own_feats
    for step in range(1, far):
        if step == 2:
            up, down, other_table = lax.optimization_barrier((up, down, other_table))
        if step == 3:
            up, down, mask, grad_hidden = lax.optimization_barrier((up, down, mask, grad_hidden))
        if step == min(3, far - 1):
            tile_late = lax.optimization_barrier((tile_own, up, down))[0]
            sent_rows, flipped_own, sent_flipped = call(
                split_kernel,
                [struct((slots, half, block), BF16)] * 3,
                (place,),
                (tile_late,),
                (pltpu.VMEM((block, block), BF16),),
            )
            tile_other = other_core(sent_rows)
        if step % 2:
            up, down = along_ring(up, order, 1), along_ring(down, order, -1)
        else:
            down, up = along_ring(down, order, -1), along_ring(up, order, 1)
        arrived += [(size - step, 0, up), (step, 0, down)]
    tables = (place, own_table, other_table)
    arrived += [(far, cut, along_ring(down[cut:], order, -1))]
    arrived += [(far, 0, along_ring(up[:cut], order, 1))]
    source_rows = call(
        functools.partial(pick_kernel, size, [item[:2] for item in arrived]),
        struct((2 * slots, half, width), BF16),
        tables,
        [piece for _, _, piece in arrived],
    )
    other_rows = other_core(source_rows)
    flipped_other = other_core(lax.optimization_barrier((sent_flipped, other_rows))[0])

    hidden, packed, kept = call(
        middle_kernel,
        [
            struct((half, inner), BF16),
            struct((half + width, width), BF16),
            struct((width // 2, width), F32),
        ],
        tables,
        (
            tile_own,
            tile_other,
            source_rows,
            other_rows,
            msg_weight,
            mask,
            expert_up,
            grad_hidden,
        ),
        (
            pltpu.VMEM((2 * slots, block, width), BF16),
            pltpu.VMEM((half, experts * width), BF16),
        ),
        flops=4 * half * width * (slots * block + experts * inner),
    )
    other_packed = other_core(packed)

    whole = struct((half, width), BF16)
    near = [far - 1, size - far + 1]
    products, up, down, mine, *terms = call(
        functools.partial(product_kernel, size, near),
        [
            struct((2 * slots, half, width), F32),
            struct((cut, width), BF16),
            struct((half - cut, width), BF16),
            struct((width // 2, width), BF16),
            whole,
            whole,
        ],
        tables,
        (flipped_own, flipped_other, packed, other_packed, kept),
        (pltpu.VMEM((block, width), BF16),),
        flops=4 * half * width * slots * block,
    )
    up, down = along_ring(up, order, 1), along_ring(down, order, -1)
    products = lax.optimization_barrier((products, up, down))[0]
    keys = [0]
    for step in range(far - 2, 0, -1):
        keys += [step, size - step]
    terms += call(
        functools.partial(spread_kernel, size, keys),
        [struct((half, width), F32 if key == 0 else BF16) for key in keys],
        tables,
        (products,),
    )
    terms = dict(zip(near + keys, terms, strict=True))

    def added(mine, theirs):
        values = [mine.astype(F32)] + [item.astype(F32) for item in theirs]
        while len(values) > 1:
            values = [values[i] + values[i + 1] for i in range(0, len(values), 2)]
        return values[0]

    def joined(received, term):
        return (received.astype(F32) + term.astype(F32)).astype(BF16)

    swaps = [(1, 2, 3)] + [(1 << bit,) for bit in range(2, size.bit_length() - 1)]
    theirs = [swapped(mine, distance) for distance in swaps.pop(0)]
    total = None
    up, down = jnp.pad(up, ((0, half - cut), (0, 0))), jnp.pad(down, ((cut, 0), (0, 0)))
    for step in range(far - 1, 0, -1):
        up, down = joined(up, terms[step]), joined(down, terms[size - step])
        if step < far - 1 and total is None:
            behind = (up, down) if step < far - 2 else (terms[step], terms[size - step])
            *theirs, _, _ = lax.optimization_barrier((*theirs, *behind))
            total = added(mine, theirs)
            if swaps:
                mine, total = total.astype(BF16), None
                theirs = [swapped(mine, distance) for distance in swaps.pop(0)]
            else:
                other_total = other_core(total)
        if step % 2:
            down, up = along_ring(down, order, -1), along_ring(up, order, 1)
        else:
            up, down = along_ring(up, order, 1), along_ring(down, order, -1)
        if step == far - 1:
            hidden = lax.optimization_barrier((hidden, up))[0]

    updated = call(
        update_kernel,
        struct((half, width), BF16),
        (),
        (mask, hidden, expert_down, own_feats),
        flops=2 * experts * half * width * inner,
    )
    msg_weight_grad = call(
        weight_kernel, struct((width, width), F32), (place,), (total, other_total)
    )
    feats_grad = call(
        finish_kernel,
        struct((half, width), BF16),
        (),
        (terms[0], up, down, msg_weight, out_grad),
        flops=2 * half * width * width,
    )
    return (updated, feats_grad, msg_weight_grad)


def solution(mesh):
    return jax.shard_map(
        per_device,
        mesh=mesh,
        in_specs=(
            P(("groups", "grid"), None),
            P(),
            P(("groups", "grid"), "rep", None, None, None),
            P(("groups", "grid"), "rep", None),
            P(("groups", "grid"), "rep", None),
            P(("groups", "grid")),
            P(),
            P(),
            P(("groups", "grid", "rep"), None),
        ),
        out_specs=(
            P(("groups", "grid", "rep"), None),
            P(("groups", "grid", "rep"), None),
            P("groups", None),
        ),
        check_vma=False,
    )
```
